32 devices in a mesh: ctx: 8 (over y, x, core), tp: 4 (over z).
Axes of the slice: x: 2, y: 2, z: 4, core: 2. Of those that a mesh axis runs over, the one named last changes fastest.
Arguments:
- positions: int32 [1280], replicated, may hold values from 0 to 1279, as said below
- queries: bfloat16 [1280, 8192], P('ctx', 'tp'), may hold values from -6 to 6
- key_state_rows: bfloat16 [1280, 1024], P('ctx', 'tp'), may hold values from -6 to 6
- value_state_rows: bfloat16 [1280, 1024], P('ctx', 'tp'), may hold values from -6 to 6
- attn_output: bfloat16 [1280, 8192], P('ctx', 'tp'), may hold values from -6 to 6
- output_grad: bfloat16 [1280, 8192], P('ctx', 'tp'), may hold values from -48 to 48
- log_sums: float32 [1280, 64], P('ctx', 'tp')
Outputs:
- query_grad: bfloat16 [1280, 8192], P('ctx', 'tp')
- key_state_gradient: bfloat16 [1280, 1024], P(('ctx', 'tp'))
- value_state_gradient: bfloat16 [1280, 1024], P(('ctx', 'tp'))
The draws below stay inside these ranges and needn't reach their ends.
Inputs may be any that keep to these rules, and one draw needn't show every extreme that they name: A permutation of 0 to 1279; each aligned block of 160 rows holds two runs of 80 rising consecutive positions, the first starting at c * (80) and the second at (15 - c) * 80, for a c of its own.
All inputs are finite; a program needn't handle non-finite values.
Results may differ from the reference program's by a relative error of at most 0.0059.
Values may be sent and summed in bfloat16 or wider, within the bound.
No kernel may reach another device: no remote copies, remote signals or barrier semaphores. Data moves between devices by JAX's collectives and lax.ppermute only.
A program may use at most 128 MiB of HBM per device.

```python
import math
import jax
import jax.numpy as jnp
from jax import lax

HEAD_SIZE = 128
QUERY_HEADS = 64
KEY_VALUE_HEADS = 8
TOK_DEV = 160
SEQUENCE_TOKENS = 1280


def paired_positions(key):
    pair_count = SEQUENCE_TOKENS // TOK_DEV
    half_rows = TOK_DEV // 2
    order = jax.random.permutation(key, pair_count).astype(jnp.int32)
    halves = jnp.stack([order, 2 * pair_count - 1 - order], axis=1)
    within = jnp.arange(half_rows, dtype=jnp.int32)
    spots = halves[:, :, None] * half_rows + within[None, None, :]
    return spots.reshape(SEQUENCE_TOKENS).astype(jnp.int32)


def draw_positions(key, part):
    return paired_positions(key)


def draw_log_sums(key, part):
    spots = paired_positions(key)
    key = jax.random.fold_in(key, 7)
    noise = jax.random.uniform(key, (SEQUENCE_TOKENS, QUERY_HEADS), jnp.float32, -0.3, 0.3)
    return jnp.log(spots.astype(jnp.float32) + 1.0)[:, None] + 0.5 + noise


def block_scale(stream_key, dims, split, least, largest):
    def one(dim, parts):
        draws = jax.random.uniform(jax.random.fold_in(jax.random.fold_in(stream_key, 6), dim), (parts,), jnp.float32, least / len(split), largest / len(split))
        return jnp.repeat(jnp.exp(draws), dims[dim] // parts).reshape((-1,) + (1,) * (len(dims) - dim - 1))

    gain = one(*split[0])
    for cut in split[1:]:
        gain = gain * one(*cut)
    return gain


def scatter_about(key, dims, width, reach, split=(), held_as=jnp.bfloat16):
    values = jax.random.normal(key, dims, jnp.float32) * width
    if len(split) > 0:
        values = block_scale(key, dims, split, -0.22, 0.18) * values
    return jnp.clip(values, min=-reach, max=reach).astype(held_as)


def setup_inputs(seed: int = 0) -> dict:
    keys = jax.random.split(jax.random.key(seed), 8)
    positions = draw_positions(jax.random.fold_in(keys[7], 71), 0)
    queries = scatter_about(keys[1], (SEQUENCE_TOKENS, QUERY_HEADS * HEAD_SIZE), 1.0, 6.0, ((0, 8), (1, 4)))
    key_state_rows = scatter_about(keys[2], (SEQUENCE_TOKENS, KEY_VALUE_HEADS * HEAD_SIZE), 1.0, 6.0, ((0, 8), (1, 4)))
    value_state_rows = scatter_about(keys[3], (SEQUENCE_TOKENS, KEY_VALUE_HEADS * HEAD_SIZE), 1.0, 6.0, ((0, 8), (1, 4)))
    attn_output = scatter_about(keys[4], (SEQUENCE_TOKENS, QUERY_HEADS * HEAD_SIZE), 1.0, 6.0, ((0, 8), (1, 4)))
    output_grad = scatter_about(keys[5], (SEQUENCE_TOKENS, QUERY_HEADS * HEAD_SIZE), 8.0, 48.0, ((0, 8), (1, 4)))
    log_sums = draw_log_sums(jax.random.fold_in(keys[7], 71), 0)
    return {"positions": positions, "queries": queries, "key_state_rows": key_state_rows, "value_state_rows": value_state_rows, "attn_output": attn_output, "output_grad": output_grad, "log_sums": log_sums}


def reference(positions, queries, key_state_rows, value_state_rows, attn_output, output_grad, log_sums):
    score_scale = 1.0 / math.sqrt(HEAD_SIZE)
    queries_per_group = QUERY_HEADS // KEY_VALUE_HEADS
    visible = positions[None, :] <= positions[:, None]

    def head_grads(head):
        group_index = head // queries_per_group
        query_head = lax.dynamic_slice_in_dim(queries, head * HEAD_SIZE, HEAD_SIZE, 1)
        key_head = lax.dynamic_slice_in_dim(key_state_rows, group_index * HEAD_SIZE, HEAD_SIZE, 1)
        value_head = lax.dynamic_slice_in_dim(value_state_rows, group_index * HEAD_SIZE, HEAD_SIZE, 1)
        out_head = lax.dynamic_slice_in_dim(attn_output, head * HEAD_SIZE, HEAD_SIZE, 1)
        grad_head = lax.dynamic_slice_in_dim(output_grad, head * HEAD_SIZE, HEAD_SIZE, 1)
        lse_head = lax.dynamic_slice_in_dim(log_sums, head, 1, 1)
        scores = jnp.dot(query_head, key_head.T, preferred_element_type=jnp.float32) * score_scale
        probs = jnp.where(visible, jnp.exp(scores - lse_head), jnp.float32(0.0))
        probs_low = probs.astype(jnp.bfloat16)
        value_part = jnp.dot(probs_low.T, grad_head, preferred_element_type=jnp.float32)
        prob_grad = jnp.dot(grad_head, value_head.T, preferred_element_type=jnp.float32)
        delta = lax.optimization_barrier(jnp.sum(grad_head.astype(jnp.float32) * out_head.astype(jnp.float32), axis=1, keepdims=True))
        score_grad = (probs * (prob_grad - delta)).astype(jnp.bfloat16)
        query_part = jnp.dot(score_grad, key_head, preferred_element_type=jnp.float32) * score_scale
        key_part = jnp.dot(score_grad.T, query_head, preferred_element_type=jnp.float32) * score_scale
        return (query_part, key_part, value_part)
    query_parts, key_part_list, value_part_list = lax.map(head_grads, jnp.arange(QUERY_HEADS, dtype=jnp.int32))
    query_grad = jnp.transpose(query_parts, (1, 0, 2)).reshape(SEQUENCE_TOKENS, QUERY_HEADS * HEAD_SIZE).astype(jnp.bfloat16)
    key_gradient_sum = lax.optimization_barrier(jnp.sum(key_part_list.reshape(KEY_VALUE_HEADS, queries_per_group, SEQUENCE_TOKENS, HEAD_SIZE), axis=1))
    value_gradient_sum = lax.optimization_barrier(jnp.sum(value_part_list.reshape(KEY_VALUE_HEADS, queries_per_group, SEQUENCE_TOKENS, HEAD_SIZE), axis=1))
    key_state_gradient = jnp.transpose(key_gradient_sum, (1, 0, 2)).reshape(SEQUENCE_TOKENS, KEY_VALUE_HEADS * HEAD_SIZE).astype(jnp.bfloat16)
    value_state_gradient = jnp.transpose(value_gradient_sum, (1, 0, 2)).reshape(SEQUENCE_TOKENS, KEY_VALUE_HEADS * HEAD_SIZE).astype(jnp.bfloat16)
    return (query_grad, key_state_gradient, value_state_gradient)
```

```python
import functools
import math

import jax
import jax.numpy as jnp
from jax import lax
from jax.experimental import pallas as pl
from jax.experimental.pallas import tpu as pltpu
from jax.sharding import PartitionSpec as P

HEAD_SIZE = 128
SCALE = 1.0 / math.sqrt(HEAD_SIZE)
EXP2_SCALE = SCALE * math.log2(math.e)
LOG2E = math.log2(math.e)
F32 = jnp.float32
BF16 = jnp.bfloat16
VMEM = pl.BlockSpec(memory_space=pltpu.VMEM)
SMEM = pl.BlockSpec(memory_space=pltpu.SMEM)


def call(kernel, outs, ins, scratch=(), smem=0):
    specs = [SMEM] * smem + [VMEM] * (len(ins) - smem)
    return pl.pallas_call(
        kernel,
        in_specs=specs,
        out_specs=[VMEM] * len(outs),
        out_shape=[jax.ShapeDtypeStruct(shape, dtype) for shape, dtype in outs],
        scratch_shapes=list(scratch),
        compiler_params=pltpu.CompilerParams(vmem_limit_bytes=48 * 2**20),
    )(*ins)


def nt(a, b):
    return lax.dot_general(a, b, (((1,), (1,)), ((), ())), preferred_element_type=F32)


def parity():
    return lax.rem(lax.axis_index("ctx"), 2)


def pack_kv_kernel(k_ref, v_ref, same_ref, other_ref):
    rows = k_ref.shape[0]
    c = parity()
    for ref, group in ((same_ref, c), (other_ref, 1 - c)):
        cols = pl.ds(pl.multiple_of(group * HEAD_SIZE, HEAD_SIZE), HEAD_SIZE)
        ref[:rows] = k_ref[:, cols]
        ref[rows:] = v_ref[:, cols]


def split_bf16(x, terms):
    parts = []
    for _ in range(terms):
        part = x.astype(BF16)
        parts.append(part)
        x = x - part.astype(F32)
    return parts


def pack_q_kernel(heads, q_ref, g_ref, o_ref, l_ref, same_ref, other_ref, same_rows, other_rows):
    rows = q_ref.shape[0]
    half = rows // 2
    c = parity()
    ones = jnp.ones((8, HEAD_SIZE), BF16)
    ones_l = jnp.ones((8, l_ref.shape[1]), BF16)
    lane = lax.broadcasted_iota(jnp.int32, (half, l_ref.shape[1]), 1)
    for ref, row_ref, group in ((same_ref, same_rows, c), (other_ref, other_rows, 1 - c)):
        for w in range(2):
            r = slice(w * half, (w + 1) * half)
            lse = jnp.clip(l_ref[r], -1e30, 1e30)
            deltas = []
            logs = []
            for h in range(heads):
                cols = pl.ds(
                    pl.multiple_of((group * heads + h) * HEAD_SIZE, HEAD_SIZE), HEAD_SIZE
                )
                g = g_ref[r, cols]
                ref[w, h * half : (h + 1) * half, :] = q_ref[r, cols]
                ref[2 + w, h * half : (h + 1) * half, :] = g
                deltas.append(g.astype(F32) * o_ref[r, cols].astype(F32))
                logs.append(jnp.where(lane == group * heads + h, lse, 0.0))
            delta = jnp.concatenate(deltas, axis=0)
            log = jnp.concatenate(logs, axis=0)
            delta_row = sum(nt(ones, part) for part in split_bf16(delta, 2))
            log_row = sum(nt(ones_l, part) for part in split_bf16(log, 3))
            row_ref[w : w + 1, :] = log_row[0:1] * LOG2E
            row_ref[2 + w : 3 + w, :] = delta_row[0:1]


def run_starts(pos_ref, tokens, shift):
    ctx = lax.axis_index("ctx")
    return pos_ref[jnp.bitwise_xor(ctx, shift) * tokens]


def steps(base, half, block, step):
    full = lax.div(base + 1, block)
    last = lax.div(base + half + block - 1, block)

    def run(masked):
        def body(t, carry):
            step(t, masked)
            return carry

        return body

    lax.fori_loop(0, full, run(False), 0)
    lax.fori_loop(full, last, run(True), 0)


def sort_keys(pos_ref, pieces, ks, vs):
    tokens = pieces[0].shape[0] // 2
    half = tokens // 2
    total = ks.shape[0]
    for m, piece in enumerate(pieces):
        first = run_starts(pos_ref, tokens, m)
        for w, start in enumerate((first, total - half - first)):
            r = pl.ds(pl.multiple_of(start, half), half)
            ks[r, :] = piece[w * half : (w + 1) * half, :]
            vs[r, :] = piece[tokens + w * half : tokens + (w + 1) * half, :]


def kv_grad_kernel(n, block, pos_ref, own, sib, own_rows, sib_rows, *refs):
    pieces, refs = refs[:n], refs[n:]
    outs, (ks, vs, dk, dv) = refs[:n], refs[n:]
    tokens = pieces[0].shape[0] // 2
    half = tokens // 2
    total = ks.shape[0]
    lanes = own.shape[1]
    sort_keys(pos_ref, pieces, ks, vs)
    dk[...] = jnp.zeros_like(dk)
    dv[...] = jnp.zeros_like(dv)
    key_row = lax.broadcasted_iota(jnp.int32, (block, lanes), 0)
    query_row = lax.rem(lax.broadcasted_iota(jnp.int32, (block, lanes), 1), half)
    ahead = query_row - key_row
    for b, (stack, vec) in enumerate(((own, own_rows), (sib, sib_rows))):
        first = run_starts(pos_ref, tokens, b)
        for w, base in enumerate((first, total - half - first)):

            def step(t, masked, stack=stack, vec=vec, w=w, base=base):
                start = pl.multiple_of(t * block, block)
                r = pl.ds(start, block)
                s = nt(ks[r, :], stack[w])
                dp = nt(vs[r, :], stack[2 + w])
                p = jnp.exp2(s * EXP2_SCALE - vec[w : w + 1, :])
                if masked:
                    p = jnp.where(ahead >= start - base, p, 0.0)
                ds = (p * (dp - vec[2 + w : 3 + w, :])).astype(BF16)
                dv[r, :] += jnp.dot(p.astype(BF16), stack[2 + w], preferred_element_type=F32)
                dk[r, :] += jnp.dot(ds, stack[w], preferred_element_type=F32)

            steps(base, half, block, step)
    for m, out in enumerate(outs):
        first = run_starts(pos_ref, tokens, m)
        for w, start in enumerate((first, total - half - first)):
            r = pl.ds(pl.multiple_of(start, half), half)
            out[w * half : (w + 1) * half, :] = (dk[r, :] * SCALE).astype(out.dtype)
            out[tokens + w * half : tokens + (w + 1) * half, :] = dv[r, :].astype(out.dtype)


def q_grad_kernel(n, block, pos_ref, own, sib, own_rows, sib_rows, *refs):
    pieces, refs = refs[:n], refs[n:]
    outs, (ks, vs, acc) = refs[:2], refs[2:]
    tokens = pieces[0].shape[0] // 2
    half = tokens // 2
    total = ks.shape[0]
    lanes = own.shape[1]
    sort_keys(pos_ref, pieces, ks, vs)
    key_row = lax.broadcasted_iota(jnp.int32, (block, lanes), 0)
    query_row = lax.rem(lax.broadcasted_iota(jnp.int32, (block, lanes), 1), half)
    ahead = query_row - key_row
    for b, (stack, vec) in enumerate(((own, own_rows), (sib, sib_rows))):
        first = run_starts(pos_ref, tokens, b)
        for w, base in enumerate((first, total - half - first)):
            acc[...] = jnp.zeros_like(acc)

            def step(t, masked, stack=stack, vec=vec, w=w, base=base):
                start = pl.multiple_of(t * block, block)
                r = pl.ds(start, block)
                k = ks[r, :]
                s = nt(k, stack[w])
                dp = nt(vs[r, :], stack[2 + w])
                p = jnp.exp2(s * EXP2_SCALE - vec[w : w + 1, :])
                if masked:
                    p = jnp.where(ahead >= start - base, p, 0.0)
                ds = (p * (dp - vec[2 + w : 3 + w, :])).astype(BF16)
                acc[...] += lax.dot_general(
                    ds, k, (((0,), (0,)), ((), ())), preferred_element_type=F32
                )

            steps(base, half, block, step)
            outs[b][w] = (acc[...] * SCALE).astype(BF16)


def sum_kernel(n, tp_count, own_ref, *refs):
    parts, refs = refs[: n - 1], refs[n - 1 :]
    outs, (total,) = refs[:tp_count], refs[tp_count:]
    tokens = own_ref.shape[0] // 2
    share = tokens // tp_count
    c = parity()
    z = lax.axis_index("tp")
    for odd in range(2):
        terms = [parts[m - 1] for m in range(1, n) if m % 2 == odd]
        value = own_ref[...] if odd == 0 else None
        for term in terms:
            term = term[...].astype(F32)
            value = term if value is None else value + term
        group = c if odd == 0 else 1 - c
        cols = pl.ds(pl.multiple_of(group * HEAD_SIZE, HEAD_SIZE), HEAD_SIZE)
        total[:, cols] = value
    for m, out in enumerate(outs):
        start = jnp.bitwise_xor(z, m) * share
        for kind in range(2):
            r = pl.ds(pl.multiple_of(kind * tokens + start, 8), share)
            out[kind] = total[r, :].astype(BF16)


def spread_kernel(tp_count, *refs):
    parts, (key_out, value_out) = refs[:tp_count], refs[tp_count:]
    z = lax.axis_index("tp")
    width = parts[0].shape[2]
    for m, part in enumerate(parts):
        cols = pl.ds(pl.multiple_of(jnp.bitwise_xor(z, m) * width, width), width)
        key_out[:, cols] = part[0]
        value_out[:, cols] = part[1]


def unstack_kernel(heads, own, other, out):
    half = out.shape[0] // 2
    c = parity()
    for ref, group in ((own, c), (other, 1 - c)):
        for w in range(2):
            for h in range(heads):
                cols = pl.ds(
                    pl.multiple_of((group * heads + h) * HEAD_SIZE, HEAD_SIZE), HEAD_SIZE
                )
                out[w * half : (w + 1) * half, cols] = ref[w, h * half : (h + 1) * half, :]


def swap(x, axis, shift):
    count = lax.axis_size(axis)
    return lax.ppermute(x, axis, [(i, i ^ shift) for i in range(count)])


def on_device(positions, queries, keys, values, attn_output, output_grad, log_sums):
    n = lax.axis_size("ctx")
    tp_count = lax.axis_size("tp")
    tokens = queries.shape[0]
    half = tokens // 2
    heads = log_sums.shape[1] // 2
    total = tokens * n
    lanes = heads * half
    block = 4 * half

    piece = ((2 * tokens, HEAD_SIZE), BF16)
    kv_same, kv_other = call(pack_kv_kernel, [piece] * 2, [keys, values])
    pieces = [kv_same] + [swap(kv_other if m % 2 else kv_same, "ctx", m) for m in range(1, n)]

    stack = ((4, lanes, HEAD_SIZE), BF16)
    vectors = ((4, lanes), F32)
    own, other, own_rows, other_rows = call(
        functools.partial(pack_q_kernel, heads),
        [stack, stack, vectors, vectors],
        [queries, output_grad, attn_output, log_sums],
    )
    sib, sib_rows = swap(other, "ctx", 1), swap(other_rows, "ctx", 1)

    operands = [positions, own, sib, own_rows, sib_rows] + pieces
    key_scratch = [pltpu.VMEM((total, HEAD_SIZE), BF16)] * 2
    partials = call(
        functools.partial(kv_grad_kernel, n, block),
        [(piece[0], F32)] + [piece] * (n - 1),
        operands,
        key_scratch + [pltpu.VMEM((total, HEAD_SIZE), F32)] * 2,
        smem=1,
    )
    received = [swap(partials[m], "ctx", m) for m in range(1, n)]

    half_stack = ((2, lanes, HEAD_SIZE), BF16)
    dq_own, dq_sib = call(
        functools.partial(q_grad_kernel, n, block),
        [half_stack] * 2,
        operands,
        key_scratch + [pltpu.VMEM((lanes, HEAD_SIZE), F32)],
        smem=1,
    )
    dq_other = swap(dq_sib, "ctx", 1)
    (query_grad,) = call(
        functools.partial(unstack_kernel, heads), [(queries.shape, BF16)], [dq_own, dq_other]
    )

    share = ((2, tokens // tp_count, 2 * HEAD_SIZE), BF16)
    shares = call(
        functools.partial(sum_kernel, n, tp_count),
        [share] * tp_count,
        [partials[0]] + received,
        [pltpu.VMEM((2 * tokens, 2 * HEAD_SIZE), F32)],
    )
    shares = [shares[0]] + [swap(shares[m], "tp", m) for m in range(1, tp_count)]
    final = ((tokens // tp_count, 2 * HEAD_SIZE * tp_count), BF16)
    key_grad, value_grad = call(
        functools.partial(spread_kernel, tp_count), [final] * 2, shares
    )
    return (query_grad, key_grad, value_grad)


def solution(mesh):
    split = P("ctx", "tp")
    rows = P(("ctx", "tp"), None)
    return jax.shard_map(
        on_device,
        mesh=mesh,
        in_specs=(P(), split, split, split, split, split, split),
        out_specs=(split, rows, rows),
        check_vma=False,
    )
```

```python
import functools
import math

import jax
import jax.numpy as jnp
from jax import lax
from jax.experimental import pallas as pl
from jax.experimental.pallas import tpu as pltpu
from jax.sharding import PartitionSpec as P

HEAD_SIZE = 128
SCALE = 1.0 / math.sqrt(HEAD_SIZE)
EXP2_SCALE = SCALE * math.log2(math.e)
FLOPS_PER_US = 1.1e9
LOG2E = math.log2(math.e)
F32 = jnp.float32
BF16 = jnp.bfloat16
VMEM = pl.BlockSpec(memory_space=pltpu.VMEM)
ANY = pl.BlockSpec(memory_space=pl.ANY)
HBM = pl.BlockSpec(memory_space=pltpu.HBM)
SMEM = pl.BlockSpec(memory_space=pltpu.SMEM)


def call(kernel, outs, ins, scratch=(), smem=0, cost=0.1, far=(), after=()):
    ins = list(ins) + [pltpu.with_memory_space_constraint(x, pltpu.HBM) for x in far]
    specs = [SMEM] * smem + [VMEM] * (len(ins) - smem - len(far))
    specs += [HBM] * len(far) + [ANY] * len(after)
    moved = sum(x.size * x.dtype.itemsize for x in ins)
    count = len(ins)
    ins = list(ins) + list(after)

    def body(*refs):
        kernel(*refs[:count], *refs[len(ins) :])

    return pl.pallas_call(
        body,
        cost_estimate=pl.CostEstimate(
            flops=int(cost * FLOPS_PER_US), bytes_accessed=moved, transcendentals=0
        ),
        in_specs=specs,
        out_specs=[VMEM] * len(outs),
        out_shape=[jax.ShapeDtypeStruct(shape, dtype) for shape, dtype in outs],
        scratch_shapes=list(scratch),
        compiler_params=pltpu.CompilerParams(vmem_limit_bytes=48 * 2**20),
    )(*ins)


def nt(a, b):
    return lax.dot_general(a, b, (((1,), (1,)), ((), ())), preferred_element_type=F32)


def parity():
    return lax.rem(lax.axis_index("ctx"), 2)


def columns(head):
    return pl.ds(pl.multiple_of(head * HEAD_SIZE, HEAD_SIZE), HEAD_SIZE)


def copy_all(pairs, sems):
    copies = [
        pltpu.make_async_copy(src, dst, sems.at[i]) for i, (src, dst) in enumerate(pairs)
    ]
    for each in copies:
        each.start()
    for each in copies:
        each.wait()


def pack_kv_kernel(k_hbm, v_hbm, same, other, sems):
    rows = k_hbm.shape[0]
    c = parity()
    pairs = [
        (src.at[:, columns(group)], ref.at[pl.ds(kind * rows, rows), :])
        for ref, group in ((other, 1 - c), (same, c))
        for kind, src in enumerate((k_hbm, v_hbm))
    ]
    copy_all(pairs, sems)


def run_starts(pos_ref, tokens, shift):
    ctx = lax.axis_index("ctx")
    return pos_ref[jnp.bitwise_xor(ctx, shift) * tokens]


def pack_q_kernel(heads, q_hbm, g_hbm, o_hbm, pos_hbm, out, larger, pos, sems):
    tokens = q_hbm.shape[0]
    half = tokens // 2
    group = 1 - parity()
    pairs = [(pos_hbm, pos)] + [
        (
            src.at[pl.ds(w * half, half), columns(group * heads + h)],
            out.at[2 * kind + w, pl.ds(h * half, half), :],
        )
        for kind, src in enumerate((q_hbm, g_hbm, o_hbm))
        for w in range(2)
        for h in range(heads)
    ]
    copy_all(pairs, sems)
    for m in range(larger.shape[0] // 2):
        for b in range(2):
            flag = jnp.where(run_starts(pos, tokens, m) > run_starts(pos, tokens, b), 1.0, 0.0)
            larger[2 * m + b : 2 * m + b + 1, :] = jnp.full((1, HEAD_SIZE), flag, F32)


def split_bf16(x, terms):
    parts = []
    for _ in range(terms):
        part = x.astype(BF16)
        parts.append(part)
        x = x - part.astype(F32)
    return parts


def rows_kernel(heads, q_ref, g_ref, o_ref, own_log, sib, sib_log, kv, *refs):
    out, own, own_t, sib_t, kv_out = refs
    lanes = own.shape[1]
    half = lanes // heads
    c = parity()
    ones = jnp.ones((8, HEAD_SIZE), BF16)
    groups, tokens = own_log.shape
    token = lax.broadcasted_iota(jnp.int32, (tokens, lanes), 0)
    lane = lax.broadcasted_iota(jnp.int32, (tokens, lanes), 1)
    head = lax.broadcasted_iota(jnp.int32, (groups, lanes), 0)
    wanted = lax.div(lax.broadcasted_iota(jnp.int32, (groups, lanes), 1), half) + c * heads

    def stacked(ref, w):
        r = slice(w * half, (w + 1) * half)
        return jnp.concatenate([ref[r, columns(c * heads + h)] for h in range(heads)], axis=0)

    for b, (log, turned) in enumerate(((own_log, own_t), (sib_log, sib_t))):
        parts = split_bf16(jnp.clip(log[...], -1e30, 1e30), 3)
        for w in range(2):
            if b == 0:
                q, g, o = (stacked(ref, w) for ref in (q_ref, g_ref, o_ref))
                own[w] = q
                own[2 + w] = g
            else:
                q, g, o = (sib[2 * kind + w] for kind in range(3))
            turned[w] = q.T
            turned[2 + w] = g.T
            place = jnp.where(token == lax.rem(lane, half) + w * half, 1.0, 0.0).astype(BF16)
            spread = sum(jnp.dot(part, place, preferred_element_type=F32) for part in parts)
            row = jnp.sum(jnp.where(head == wanted, spread, 0.0), axis=0, keepdims=True)
            out[4 * b + w : 4 * b + w + 1, :] = row * LOG2E
            delta = g.astype(F32) * o.astype(F32)
            row = sum(nt(ones, part) for part in split_bf16(delta, 2))
            out[4 * b + 2 + w : 4 * b + 3 + w, :] = row[0:1]
    kv_out[...] = kv[...]


def seen_in_run(half, lanes):
    key_row = lax.broadcasted_iota(jnp.int32, (half, lanes), 0)
    query_row = lax.rem(lax.broadcasted_iota(jnp.int32, (half, lanes), 1), half)
    return key_row <= query_row


def probs_and_grads(k, v, turned, vec, at, which, mask=None):
    s = jnp.dot(k, turned[which], preferred_element_type=F32)
    p = jnp.exp2(s * EXP2_SCALE - vec[pl.ds(at + which, 1), :])
    if mask is not None:
        p = jnp.where(mask, p, 0.0)
    dp = jnp.dot(v, turned[2 + which], preferred_element_type=F32)
    return p, (p * (dp - vec[pl.ds(at + 2 + which, 1), :])).astype(BF16)


def first_runs(piece, tokens, half):
    rows = piece.shape[0] // 2

    def both(at):
        return jnp.concatenate(
            [piece[at + a * tokens : at + a * tokens + half, :] for a in range(2)], axis=0
        )

    return both(0), both(rows)


def one_run(piece, tokens, half, a, which):
    at = a * tokens + which * half
    if not isinstance(which, int):
        at = pl.multiple_of(at, half)
    rows = piece.shape[0] // 2
    return piece[pl.ds(at, half), :], piece[pl.ds(rows + at, half), :]


def is_larger(larger, pair, a, b):
    at = 4 * pair + 2 * a + b
    return jnp.max(larger[at : at + 1, :]) > 0.5


def kv_grad_kernel(pair, larger, own, sib, own_t, sib_t, vec, piece, out):
    tokens = piece.shape[0] // 4
    half = tokens // 2
    rows = 2 * tokens
    sides = ((own, own_t), (sib, sib_t))

    def terms(k, v, b, which, mask=None):
        stack, turned = sides[b]
        p, ds = probs_and_grads(k, v, turned, vec, 4 * b, which, mask)
        return (
            jnp.dot(ds, stack[which], preferred_element_type=F32),
            jnp.dot(p.astype(BF16), stack[2 + which], preferred_element_type=F32),
        )

    sums = {(a, w): [] for a in range(2) for w in range(2)}
    k, v = first_runs(piece, tokens, half)
    for b in range(2):
        both = terms(k, v, b, 1)
        for a in range(2):
            sums[a, 0].append([x[a * half : (a + 1) * half] for x in both])
    seen = seen_in_run(half, own.shape[1]) if pair == 0 else None
    for a in range(2):
        for b in range(2):
            if pair == 0 and a == b:
                for w in range(2):
                    k, v = one_run(piece, tokens, half, a, w)
                    sums[a, w].append(terms(k, v, b, w, seen))
                continue
            second = is_larger(larger, pair, a, b)
            which = jnp.where(second, 1, 0)
            k, v = one_run(piece, tokens, half, a, which)
            both = terms(k, v, b, which)
            sums[a, 0].append([jnp.where(second, 0.0, x) for x in both])
            sums[a, 1].append([jnp.where(second, x, 0.0) for x in both])
    for (a, w), parts in sums.items():
        at = a * tokens + w * half
        out[at : at + half, :] = (sum(x[0] for x in parts) * SCALE).astype(out.dtype)
        out[rows + at : rows + at + half, :] = sum(x[1] for x in parts).astype(out.dtype)


def q_grad_kernel(b, larger, turned, vec, *refs):
    pieces, (out, acc) = refs[:-2], refs[-2:]
    tokens = pieces[0].shape[0] // 4
    half = tokens // 2
    acc[...] = jnp.zeros_like(acc)

    def add(k, v, which, mask=None):
        _, ds = probs_and_grads(k, v, turned, vec, 4 * b, which, mask)
        acc[which] += jnp.dot(k.T, ds, preferred_element_type=F32)

    for pair, piece in enumerate(pieces):
        add(*first_runs(piece, tokens, half), 1)
        for a in range(2):
            if pair == 0 and a == b:
                seen = seen_in_run(half, turned.shape[2])
                for w in range(2):
                    add(*one_run(piece, tokens, half, a, w), w, seen)
                continue
            which = jnp.where(is_larger(larger, pair, a, b), 1, 0)
            add(*one_run(piece, tokens, half, a, which), which)
    for w in range(2):
        out[w] = (acc[w] * SCALE).T.astype(BF16)


def merge_kv_kernel(same_ref, other_ref, log, out, log_out):
    log_out[...] = log[...]
    tokens = same_ref.shape[0] // 2
    for a, ref in enumerate((same_ref, other_ref)):
        for kind in range(2):
            at = (2 * kind + a) * tokens
            out[at : at + tokens, :] = ref[kind * tokens : (kind + 1) * tokens, :]


def sum_kernel(*refs):
    parts, (same_out, other_out) = refs[:-2], refs[-2:]
    tokens = parts[0].shape[0] // 4
    for a, out in enumerate((same_out, other_out)):
        for kind in range(2):
            at = (2 * kind + a) * tokens
            value = parts[0][at : at + tokens, :]
            for part in parts[1:]:
                value = value + part[at : at + tokens, :].astype(F32)
            out[kind * tokens : (kind + 1) * tokens, :] = value.astype(BF16)


def share_kernel(tp_count, same, other, *refs):
    outs, (total,) = refs[:tp_count], refs[tp_count:]
    tokens = same.shape[0] // 2
    share = tokens // tp_count
    c = parity()
    z = lax.axis_index("tp")
    for ref, group in ((same, c), (other, 1 - c)):
        cols = pl.ds(pl.multiple_of(group * HEAD_SIZE, HEAD_SIZE), HEAD_SIZE)
        total[:, cols] = ref[...].astype(F32)
    for m, out in enumerate(outs):
        start = jnp.bitwise_xor(z, m) * share
        for kind in range(2):
            r = pl.ds(pl.multiple_of(kind * tokens + start, 8), share)
            out[kind] = total[r, :].astype(BF16)


def spread_kernel(tp_count, *refs):
    parts, (key_out, value_out) = refs[:tp_count], refs[tp_count:]
    z = lax.axis_index("tp")
    width = parts[0].shape[2]
    for m, part in enumerate(parts):
        cols = pl.ds(pl.multiple_of(jnp.bitwise_xor(z, m) * width, width), width)
        key_out[:, cols] = part[0]
        value_out[:, cols] = part[1]


def unstack_kernel(heads, own, other, out):
    half = out.shape[0] // 2
    c = parity()
    for ref, group in ((own, c), (other, 1 - c)):
        for w in range(2):
            for h in range(heads):
                cols = pl.ds(
                    pl.multiple_of((group * heads + h) * HEAD_SIZE, HEAD_SIZE), HEAD_SIZE
                )
                out[w * half : (w + 1) * half, cols] = ref[w, h * half : (h + 1) * half, :]


def swap(x, axis, shift):
    count = lax.axis_size(axis)
    return lax.ppermute(x, axis, [(i, i ^ shift) for i in range(count)])


def on_device(positions, queries, keys, values, attn_output, output_grad, log_sums):
    n = lax.axis_size("ctx")
    tp_count = lax.axis_size("tp")
    tokens = queries.shape[0]
    half = tokens // 2
    heads = log_sums.shape[1] // 2
    lanes = heads * half

    half_piece = ((2 * tokens, HEAD_SIZE), BF16)
    piece = ((4 * tokens, HEAD_SIZE), BF16)
    stack = ((6, lanes, HEAD_SIZE), BF16)
    kv_same, kv_other = call(
        pack_kv_kernel,
        [half_piece] * 2,
        [],
        [pltpu.SemaphoreType.DMA((4,))],
        far=[keys, values],
    )
    other, larger = call(
        functools.partial(pack_q_kernel, heads),
        [stack, ((2 * n, HEAD_SIZE), F32)],
        [],
        [pltpu.SMEM(positions.shape, jnp.int32), pltpu.SemaphoreType.DMA((6 * heads + 1,))],
        cost=1.0,
        far=[queries, output_grad, attn_output, positions],
        after=[kv_same],
    )
    kv_pair, other = lax.optimization_barrier((swap(kv_other, "ctx", 1), other))
    kv_chip, logs = call(
        merge_kv_kernel,
        [piece, (log_sums.T.shape, F32)],
        [kv_same, kv_pair, log_sums.T],
    )
    sib = swap(other, "ctx", 1)
    turned = ((4, HEAD_SIZE, lanes), BF16)
    vec, own, own_t, sib_t, kv_late = call(
        functools.partial(rows_kernel, heads),
        [((8, lanes), F32), ((4, lanes, HEAD_SIZE), BF16), turned, turned, piece],
        [queries, output_grad, attn_output, logs, sib, swap(logs, "ctx", 1), kv_chip],
        cost=1.0,
    )
    late = n // 2 - 1
    pieces = [kv_chip] + [
        swap(kv_late if pair == late else kv_chip, "ctx", 2 * pair) for pair in range(1, n // 2)
    ]

    def kv_grads(pair, after=()):
        (out,) = call(
            functools.partial(kv_grad_kernel, pair),
            [(piece[0], BF16 if pair else F32)],
            [larger, own, sib, own_t, sib_t, vec, pieces[pair]],
            cost=0.5,
            after=after,
        )
        return out

    partials = [kv_grads(pair) for pair in range(1, n // 2)]
    received = [swap(x, "ctx", 2 * pair + 2) for pair, x in enumerate(partials)]
    local = kv_grads(0, partials[-1:])

    def q_grads(member, member_t, after=()):
        (out,) = call(
            functools.partial(q_grad_kernel, member),
            [((2, lanes, HEAD_SIZE), BF16)],
            [larger, member_t, vec] + pieces,
            [pltpu.VMEM((2, HEAD_SIZE, lanes), F32)],
            cost=2.5,
            after=after,
        )
        return out

    dq_sib = q_grads(1, sib_t)
    dq_other = swap(dq_sib, "ctx", 1)
    sum_same, sum_other = call(
        sum_kernel, [half_piece] * 2, [local] + received, after=[dq_sib]
    )
    share = ((2, tokens // tp_count, 2 * HEAD_SIZE), BF16)
    shares = call(
        functools.partial(share_kernel, tp_count),
        [share] * tp_count,
        [sum_same, swap(sum_other, "ctx", 1)],
        [pltpu.VMEM((2 * tokens, 2 * HEAD_SIZE), F32)],
    )
    dq_own = q_grads(0, own_t, [shares[0]])
    (query_grad,) = call(
        functools.partial(unstack_kernel, heads),
        [(queries.shape, BF16)],
        [dq_own, dq_other],
        cost=1.0,
    )

    shares = [shares[0]] + [swap(shares[m], "tp", m) for m in range(1, tp_count)]
    final = ((tokens // tp_count, 2 * HEAD_SIZE * tp_count), BF16)
    key_grad, value_grad = call(
        functools.partial(spread_kernel, tp_count), [final] * 2, shares, after=[pltpu.with_memory_space_constraint(query_grad, pltpu.HBM)]
    )
    return (query_grad, key_grad, value_grad)


def solution(mesh):
    split = P("ctx", "tp")
    rows = P(("ctx", "tp"), None)
    return jax.shard_map(
        on_device,
        mesh=mesh,
        in_specs=(P(), split, split, split, split, split, split),
        out_specs=(split, rows, rows),
        check_vma=False,
    )
```

```python
import functools
import math

import jax
import jax.numpy as jnp
from jax import lax
from jax.experimental import pallas as pl
from jax.experimental.pallas import tpu as pltpu
from jax.sharding import PartitionSpec as P

HEAD_SIZE = 128
SCALE = 1.0 / math.sqrt(HEAD_SIZE)
EXP2_SCALE = SCALE * math.log2(math.e)
FLOPS_PER_US = 1.1e9
LOG2E = math.log2(math.e)
F32 = jnp.float32
BF16 = jnp.bfloat16
VMEM = pl.BlockSpec(memory_space=pltpu.VMEM)
ANY = pl.BlockSpec(memory_space=pl.ANY)
HBM = pl.BlockSpec(memory_space=pltpu.HBM)
SMEM = pl.BlockSpec(memory_space=pltpu.SMEM)


def call(kernel, outs, ins, scratch=(), smem=0, cost=0.1, far=(), after=(), out_spec=VMEM):
    ins = list(ins) + [pltpu.with_memory_space_constraint(x, pltpu.HBM) for x in far]
    specs = [SMEM] * smem + [VMEM] * (len(ins) - smem - len(far))
    specs += [HBM] * len(far) + [ANY] * len(after)
    moved = sum(x.size * x.dtype.itemsize for x in ins)
    count = len(ins)
    ins = list(ins) + list(after)

    def body(*refs):
        kernel(*refs[:count], *refs[len(ins) :])

    return pl.pallas_call(
        body,
        cost_estimate=pl.CostEstimate(
            flops=int(cost * FLOPS_PER_US), bytes_accessed=moved, transcendentals=0
        ),
        in_specs=specs,
        out_specs=[out_spec] * len(outs),
        out_shape=[jax.ShapeDtypeStruct(shape, dtype) for shape, dtype in outs],
        scratch_shapes=list(scratch),
        compiler_params=pltpu.CompilerParams(vmem_limit_bytes=48 * 2**20),
    )(*ins)


def nt(a, b):
    return lax.dot_general(a, b, (((1,), (1,)), ((), ())), preferred_element_type=F32)


def parity():
    return lax.rem(lax.axis_index("ctx"), 2)


def columns_of(head):
    return pl.ds(pl.multiple_of(head * HEAD_SIZE, HEAD_SIZE), HEAD_SIZE)


def copy_all(pairs, sems):
    copies = [
        pltpu.make_async_copy(src, dst, sems.at[i]) for i, (src, dst) in enumerate(pairs)
    ]
    for each in copies:
        each.start()
    for each in copies:
        each.wait()


def pack_kv_kernel(k_hbm, v_hbm, same, other, sems):
    rows = k_hbm.shape[0]
    c = parity()
    pairs = [
        (src.at[:, columns_of(group)], ref.at[pl.ds(kind * rows, rows), :])
        for ref, group in ((other, 1 - c), (same, c))
        for kind, src in enumerate((k_hbm, v_hbm))
    ]
    copy_all(pairs, sems)


def run_starts(pos_ref, tokens, shift):
    ctx = lax.axis_index("ctx")
    return pos_ref[jnp.bitwise_xor(ctx, shift) * tokens]


def pack_q_kernel(heads, q_hbm, g_hbm, o_hbm, pos_hbm, out, larger, pos, sems):
    tokens = q_hbm.shape[0]
    half = tokens // 2
    group = 1 - parity()
    pairs = [(pos_hbm, pos)] + [
        (
            src.at[pl.ds(w * half, half), columns_of(group * heads + h)],
            out.at[2 * kind + w, pl.ds(h * half, half), :],
        )
        for kind, src in enumerate((q_hbm, g_hbm, o_hbm))
        for w in range(2)
        for h in range(heads)
    ]
    copy_all(pairs, sems)
    for m in range(larger.shape[0] // 2):
        for b in range(2):
            flag = jnp.where(run_starts(pos, tokens, m) > run_starts(pos, tokens, b), 1.0, 0.0)
            larger[2 * m + b : 2 * m + b + 1, :] = jnp.full((1, HEAD_SIZE), flag, F32)


def split_bf16(x, terms):
    parts = []
    for _ in range(terms):
        part = x.astype(BF16)
        parts.append(part)
        x = x - part.astype(F32)
    return parts


def rows_kernel(heads, q_ref, g_ref, o_ref, own_log, sib, sib_log, kv, *refs):
    out, turned_out, own, own_t, sib_t, kv_out = refs
    lanes = own.shape[1]
    half = lanes // heads
    c = parity()
    ones = jnp.ones((8, HEAD_SIZE), BF16)
    groups, tokens = own_log.shape
    token = lax.broadcasted_iota(jnp.int32, (tokens, lanes), 0)
    lane = lax.broadcasted_iota(jnp.int32, (tokens, lanes), 1)
    head = lax.broadcasted_iota(jnp.int32, (groups, lanes), 0)
    wanted = lax.div(lax.broadcasted_iota(jnp.int32, (groups, lanes), 1), half) + c * heads

    def stacked(ref, w):
        r = slice(w * half, (w + 1) * half)
        return jnp.concatenate([ref[r, columns_of(c * heads + h)] for h in range(heads)], axis=0)

    for b, (log, turned) in enumerate(((own_log, own_t), (sib_log, sib_t))):
        parts = split_bf16(jnp.clip(log[...], -1e30, 1e30), 3)
        for w in range(2):
            if b == 0:
                q, g, o = (stacked(ref, w) for ref in (q_ref, g_ref, o_ref))
                own[w] = q
                own[2 + w] = g
            else:
                q, g, o = (sib[2 * kind + w] for kind in range(3))
            turned[w] = q.T
            turned[2 + w] = g.T
            place = jnp.where(token == lax.rem(lane, half) + w * half, 1.0, 0.0).astype(BF16)
            spread = sum(jnp.dot(part, place, preferred_element_type=F32) for part in parts)
            row = jnp.sum(jnp.where(head == wanted, spread, 0.0), axis=0, keepdims=True)
            out[4 * b + w : 4 * b + w + 1, :] = row * LOG2E
            delta = g.astype(F32) * o.astype(F32)
            row = sum(nt(ones, part) for part in split_bf16(delta, 2))
            out[4 * b + 2 + w : 4 * b + 3 + w, :] = row[0:1]
    out[8:16, :] = lax.rem(lax.broadcasted_iota(jnp.int32, (8, lanes), 1), half).astype(F32)
    turned_out[...] = out[...].T
    kv_out[...] = kv[...]


def is_larger(larger, m, b):
    return jnp.max(larger[2 * m + b : 2 * m + b + 1, :]) > 0.5


def one_run(piece, tokens, half, a, which):
    at = a * tokens + which * half
    if not isinstance(which, int):
        at = pl.multiple_of(at, half)
    rows = piece.shape[0] // 2
    return piece[pl.ds(at, half), :], piece[pl.ds(rows + at, half), :]


def kv_grad_kernel(pair, larger, own, sib, own_t, sib_t, vec, piece, out):
    tokens = piece.shape[0] // 4
    half = tokens // 2
    rows = 2 * tokens
    lanes = own.shape[1]
    stacks, turned = (own, sib), (own_t, sib_t)
    first = [one_run(piece, tokens, half, a, 0) for a in range(2)]
    k, v = (jnp.concatenate(x, axis=0) for x in zip(*first))
    jobs = [(k, v, b, 1, None) for b in range(2)]
    for a in range(2):
        for b in range(2):
            if pair == 0 and a == b:
                jobs += [(*one_run(piece, tokens, half, a, w), b, w, (a, w)) for w in range(2)]
            else:
                second = is_larger(larger, 2 * pair + a, b)
                which = jnp.where(second, 1, 0)
                run = one_run(piece, tokens, half, a, which)
                jobs.append((*run, b, which, (a, second)))
    if pair == 0:
        key_row = lax.broadcasted_iota(jnp.int32, (half, lanes), 0)
        query_row = lax.rem(lax.broadcasted_iota(jnp.int32, (half, lanes), 1), half)
        seen = key_row <= query_row

    def products(job):
        k, v, b, which, _ = job
        s = jnp.dot(k, turned[b][which], preferred_element_type=F32)
        return s, jnp.dot(v, turned[b][2 + which], preferred_element_type=F32)

    sums = {(a, w): [] for a in range(2) for w in range(2)}
    ahead = products(jobs[0])
    for i, job in enumerate(jobs):
        (s, dp), ahead = ahead, products(jobs[i + 1]) if i + 1 < len(jobs) else None
        _, _, b, which, place = job
        p = jnp.exp2(s * EXP2_SCALE - vec[pl.ds(4 * b + which, 1), :])
        if place is not None and isinstance(which, int):
            p = jnp.where(seen, p, 0.0)
        ds = (p * (dp - vec[pl.ds(4 * b + 2 + which, 1), :])).astype(BF16)
        value_term = jnp.dot(p.astype(BF16), stacks[b][2 + which], preferred_element_type=F32)
        key_term = jnp.dot(ds, stacks[b][which], preferred_element_type=F32)
        both = key_term, value_term
        if place is None:
            for a in range(2):
                sums[a, 0].append([x[a * half : (a + 1) * half] for x in both])
        elif isinstance(which, int):
            sums[place].append(both)
        else:
            a, second = place
            sums[a, 0].append([jnp.where(second, 0.0, x) for x in both])
            sums[a, 1].append([jnp.where(second, x, 0.0) for x in both])
    for (a, w), parts in sums.items():
        at = a * tokens + w * half
        out[at : at + half, :] = (sum(x[0] for x in parts) * SCALE).astype(out.dtype)
        out[rows + at : rows + at + half, :] = sum(x[1] for x in parts).astype(out.dtype)


def q_grads(b, larger, stack, columns, pieces):
    tokens = pieces[0].shape[0] // 4
    half = tokens // 2
    rows = 2 * tokens
    grads = [0.0, 0.0]
    spot = columns[:, 8:9]
    for start in range(0, len(pieces), 4):
        some = pieces[start : start + 4]

        def gather(at):
            return jnp.concatenate(
                [x[at + a * tokens : at + a * tokens + half, :] for x in some for a in range(2)],
                axis=0,
            )

        count = 2 * len(some)
        lane = lax.broadcasted_iota(jnp.int32, (1, count * half), 1)
        group = lax.div(lane, half)
        least = [lax.rem(lane, half).astype(F32)] * 2
        for i in range(count):
            m = 2 * start + i
            if m != b:
                sign = jnp.where(is_larger(larger, m, b), 1.0, -1.0) * 2 * tokens
                least[0] = jnp.where(group == i, sign, least[0])
                least[1] = jnp.where(group == i, -sign, least[1])
        runs = [(gather(at), gather(rows + at)) for at in (0, half)]
        for which, run, limit in ((0, 0, least[0]), (1, 0, None), (1, 1, least[1])):
            k, v = runs[run]
            p = jnp.exp2(
                nt(stack[which], k) * EXP2_SCALE - columns[:, 4 * b + which : 4 * b + which + 1]
            )
            if limit is not None:
                p = jnp.where(spot >= limit, p, 0.0)
            at = 4 * b + 2 + which
            ds = (p * (nt(stack[2 + which], v) - columns[:, at : at + 1])).astype(BF16)
            grads[which] = grads[which] + jnp.dot(ds, k, preferred_element_type=F32)
    return [(x * SCALE).astype(BF16) for x in grads]


def sib_grad_kernel(larger, stack, columns, *refs):
    pieces, out = refs[:-1], refs[-1]
    out[0], out[1] = q_grads(1, larger, stack, columns, pieces)


def own_grad_kernel(heads, larger, stack, columns, other, *refs):
    pieces, (out, held, sems) = refs[:-3], refs[-3:]
    half = out.shape[0] // 2
    c = parity()

    def copies(ref, group):
        return [
            pltpu.make_async_copy(
                ref.at[w, pl.ds(h * half, half), :],
                out.at[pl.ds(w * half, half), columns_of(group * heads + h)],
                sems.at[group_sems + w * heads + h],
            )
            for w in range(2)
            for h in range(heads)
        ]

    group_sems = 0
    first = copies(other, 1 - c)
    group_sems = 2 * heads
    second = copies(held, c)
    for each in first:
        each.start()
    held[0], held[1] = q_grads(0, larger, stack, columns, pieces)
    for each in second:
        each.start()
    for each in first + second:
        each.wait()


def merge_kv_kernel(same_ref, other_ref, log, out, log_out):
    log_out[...] = log[...]
    tokens = same_ref.shape[0] // 2
    for a, ref in enumerate((same_ref, other_ref)):
        for kind in range(2):
            at = (2 * kind + a) * tokens
            out[at : at + tokens, :] = ref[kind * tokens : (kind + 1) * tokens, :]


def sum_kernel(*refs):
    parts, (same_out, other_out) = refs[:-2], refs[-2:]
    tokens = parts[0].shape[0] // 4
    for a, out in enumerate((same_out, other_out)):
        for kind in range(2):
            at = (2 * kind + a) * tokens
            value = parts[0][at : at + tokens, :]
            for part in parts[1:]:
                value = value + part[at : at + tokens, :].astype(F32)
            out[kind * tokens : (kind + 1) * tokens, :] = value.astype(BF16)


def share_kernel(tp_count, same, other, *refs):
    outs, (total,) = refs[:tp_count], refs[tp_count:]
    tokens = same.shape[0] // 2
    share = tokens // tp_count
    c = parity()
    z = lax.axis_index("tp")
    for ref, group in ((same, c), (other, 1 - c)):
        cols = pl.ds(pl.multiple_of(group * HEAD_SIZE, HEAD_SIZE), HEAD_SIZE)
        total[:, cols] = ref[...].astype(F32)
    for m, out in enumerate(outs):
        start = jnp.bitwise_xor(z, m) * share
        for kind in range(2):
            r = pl.ds(pl.multiple_of(kind * tokens + start, 8), share)
            out[kind] = total[r, :].astype(BF16)


def spread_kernel(tp_count, order, *refs):
    parts, (key_out, value_out) = refs[:tp_count], refs[tp_count:]
    z = lax.axis_index("tp")
    width = parts[0].shape[2]
    for m, part in zip(order, parts):
        cols = pl.ds(pl.multiple_of(jnp.bitwise_xor(z, m) * width, width), width)
        key_out[:, cols] = part[0]
        value_out[:, cols] = part[1]


def swap(x, axis, shift):
    count = lax.axis_size(axis)
    return lax.ppermute(x, axis, [(i, i ^ shift) for i in range(count)])


def on_device(positions, queries, keys, values, attn_output, output_grad, log_sums):
    n = lax.axis_size("ctx")
    tp_count = lax.axis_size("tp")
    tokens = queries.shape[0]
    half = tokens // 2
    heads = log_sums.shape[1] // 2
    lanes = heads * half

    half_piece = ((2 * tokens, HEAD_SIZE), BF16)
    piece = ((4 * tokens, HEAD_SIZE), BF16)
    stack = ((6, lanes, HEAD_SIZE), BF16)
    kv_same, kv_other = call(
        pack_kv_kernel,
        [half_piece] * 2,
        [],
        [pltpu.SemaphoreType.DMA((4,))],
        far=[keys, values],
    )
    other, larger = call(
        functools.partial(pack_q_kernel, heads),
        [stack, ((2 * n, HEAD_SIZE), F32)],
        [],
        [pltpu.SMEM(positions.shape, jnp.int32), pltpu.SemaphoreType.DMA((6 * heads + 1,))],
        cost=1.0,
        far=[queries, output_grad, attn_output, positions],
        after=[kv_same],
    )
    kv_pair, other = lax.optimization_barrier((swap(kv_other, "ctx", 1), other))
    kv_chip, logs = call(
        merge_kv_kernel,
        [piece, (log_sums.T.shape, F32)],
        [kv_same, kv_pair, log_sums.T],
    )
    sib = swap(other, "ctx", 1)
    turned = ((4, HEAD_SIZE, lanes), BF16)
    vec, columns, own, own_t, sib_t, kv_late = call(
        functools.partial(rows_kernel, heads),
        [((16, lanes), F32), ((lanes, 16), F32), ((4, lanes, HEAD_SIZE), BF16), turned, turned, piece],
        [queries, output_grad, attn_output, logs, sib, swap(logs, "ctx", 1), kv_chip],
        cost=1.0,
    )
    late = n // 2 - 1
    pieces = {
        pair: swap(kv_late if pair == late else kv_chip, "ctx", 2 * pair)
        for pair in reversed(range(1, n // 2))
    }
    pieces = [kv_chip] + [pieces[pair] for pair in range(1, n // 2)]

    def kv_grads(pair, after=()):
        (out,) = call(
            functools.partial(kv_grad_kernel, pair),
            [(piece[0], BF16 if pair else F32)],
            [larger, own, sib, own_t, sib_t, vec, pieces[pair]],
            cost=0.5,
            after=after,
        )
        return out

    partials = {}
    for pair in reversed(range(1, late)):
        partials[pair] = kv_grads(pair, [partials[pair + 1]] if pair + 1 < late else [])
    partials[late] = kv_grads(late)
    local = kv_grads(0, [partials[late]])
    received = [swap(partials[pair], "ctx", 2 * pair) for pair in range(1, n // 2)]

    (dq_sib,) = call(
        sib_grad_kernel,
        [((2, lanes, HEAD_SIZE), BF16)],
        [larger, sib, columns] + pieces,
        cost=2.5,
        after=[local],
    )
    sum_same, sum_other = call(
        sum_kernel, [half_piece] * 2, [local] + received, after=[dq_sib]
    )
    dq_sib, sum_other = lax.optimization_barrier((dq_sib, sum_other))
    dq_other = swap(dq_sib, "ctx", 1)
    share = ((2, tokens // tp_count, 2 * HEAD_SIZE), BF16)
    shares = call(
        functools.partial(share_kernel, tp_count),
        [share] * tp_count,
        [sum_same, swap(sum_other, "ctx", 1)],
        [pltpu.VMEM((2 * tokens, 2 * HEAD_SIZE), F32)],
    )
    (query_grad,) = call(
        functools.partial(own_grad_kernel, heads),
        [(queries.shape, BF16)],
        [larger, own, columns, dq_other] + pieces,
        [pltpu.VMEM((2, lanes, HEAD_SIZE), BF16), pltpu.SemaphoreType.DMA((4 * heads,))],
        cost=3.0,
        after=[shares[0]],
        out_spec=HBM,
    )
    order = [0, *range(2, tp_count), 1]
    shares = [shares[0]] + [swap(shares[m], "tp", m) for m in order[1:]]
    final = ((tokens // tp_count, 2 * HEAD_SIZE * tp_count), BF16)
    key_grad, value_grad = call(
        functools.partial(spread_kernel, tp_count, order), [final] * 2, shares, after=[pltpu.with_memory_space_constraint(query_grad, pltpu.HBM)]
    )
    return (query_grad, key_grad, value_grad)


def solution(mesh):
    split = P("ctx", "tp")
    rows = P(("ctx", "tp"), None)
    return jax.shard_map(
        on_device,
        mesh=mesh,
        in_specs=(P(), split, split, split, split, split, split),
        out_specs=(split, rows, rows),
        check_vma=False,
    )
```

```python
import functools
import math

import jax
import jax.numpy as jnp
from jax import lax
from jax.experimental import pallas as pl
from jax.experimental.pallas import tpu as pltpu
from jax.sharding import PartitionSpec as P

HEAD_SIZE = 128
SCALE = 1.0 / math.sqrt(HEAD_SIZE)
EXP2_SCALE = SCALE * math.log2(math.e)
FLOPS_PER_US = 1.1e9
LOG2E = math.log2(math.e)
F32 = jnp.float32
BF16 = jnp.bfloat16
VMEM = pl.BlockSpec(memory_space=pltpu.VMEM)
ANY = pl.BlockSpec(memory_space=pl.ANY)
HBM = pl.BlockSpec(memory_space=pltpu.HBM)
SMEM = pl.BlockSpec(memory_space=pltpu.SMEM)


def call(kernel, outs, ins, scratch=(), smem=0, cost=0.1, far=(), after=(), out_spec=VMEM):
    ins = list(ins) + [pltpu.with_memory_space_constraint(x, pltpu.HBM) for x in far]
    specs = [SMEM] * smem + [VMEM] * (len(ins) - smem - len(far))
    specs += [HBM] * len(far) + [ANY] * len(after)
    moved = sum(x.size * x.dtype.itemsize for x in ins)
    count = len(ins)
    ins = list(ins) + list(after)

    def body(*refs):
        kernel(*refs[:count], *refs[len(ins) :])

    return pl.pallas_call(
        body,
        cost_estimate=pl.CostEstimate(
            flops=int(cost * FLOPS_PER_US), bytes_accessed=moved, transcendentals=0
        ),
        in_specs=specs,
        out_specs=[out_spec] * len(outs),
        out_shape=[jax.ShapeDtypeStruct(shape, dtype) for shape, dtype in outs],
        scratch_shapes=list(scratch),
        compiler_params=pltpu.CompilerParams(vmem_limit_bytes=48 * 2**20),
    )(*ins)


def nt(a, b):
    return lax.dot_general(a, b, (((1,), (1,)), ((), ())), preferred_element_type=F32)


def parity():
    return lax.rem(lax.axis_index("ctx"), 2)


def columns_of(head):
    return pl.ds(pl.multiple_of(head * HEAD_SIZE, HEAD_SIZE), HEAD_SIZE)


def copy_all(pairs, sems):
    copies = [
        pltpu.make_async_copy(src, dst, sems.at[i]) for i, (src, dst) in enumerate(pairs)
    ]
    for each in copies:
        each.start()
    for each in copies:
        each.wait()


def run_starts(pos_ref, tokens, shift):
    ctx = lax.axis_index("ctx")
    return pos_ref[jnp.bitwise_xor(ctx, shift) * tokens]


def pack_q_kernel(heads, q_hbm, g_hbm, pos_hbm, out, larger, pos, sems):
    tokens = q_hbm.shape[0]
    half = tokens // 2
    group = 1 - parity()
    pairs = [(pos_hbm, pos)] + [
        (
            src.at[pl.ds(w * half, half), columns_of(group * heads + h)],
            out.at[2 * kind + w, pl.ds(h * half, half), :],
        )
        for kind, src in enumerate((q_hbm, g_hbm))
        for w in range(2)
        for h in range(heads)
    ]
    copy_all(pairs, sems)
    for m in range(larger.shape[0] // 2):
        for b in range(2):
            flag = jnp.where(run_starts(pos, tokens, m) > run_starts(pos, tokens, b), 1.0, 0.0)
            larger[2 * m + b : 2 * m + b + 1, :] = jnp.full((1, HEAD_SIZE), flag, F32)


def split_bf16(x, terms):
    parts = []
    for _ in range(terms):
        part = x.astype(BF16)
        parts.append(part)
        x = x - part.astype(F32)
    return parts


def rows_kernel(heads, q_ref, g_ref, o_ref, log, sib, kv, *refs):
    own_rows, other_rows, own, own_t, sib_t, kv_out = refs
    lanes = own.shape[1]
    half = lanes // heads
    c = parity()
    ones = jnp.ones((8, HEAD_SIZE), BF16)
    groups, tokens = log.shape
    token = lax.broadcasted_iota(jnp.int32, (tokens, lanes), 0)
    lane = lax.broadcasted_iota(jnp.int32, (tokens, lanes), 1)
    head = lax.broadcasted_iota(jnp.int32, (groups, lanes), 0)
    head_of_lane = lax.div(lax.broadcasted_iota(jnp.int32, (groups, lanes), 1), half)
    logs = split_bf16(jnp.clip(log[...], -1e30, 1e30), 3)
    for w in range(2):
        r = slice(w * half, (w + 1) * half)
        place = jnp.where(token == lax.rem(lane, half) + w * half, 1.0, 0.0).astype(BF16)
        spread = sum(jnp.dot(part, place, preferred_element_type=F32) for part in logs)
        for out, group in ((own_rows, c), (other_rows, 1 - c)):
            cols = [columns_of(group * heads + h) for h in range(heads)]
            g, o = (
                jnp.concatenate([ref[r, col] for col in cols], axis=0) for ref in (g_ref, o_ref)
            )
            if out is own_rows:
                q = jnp.concatenate([q_ref[r, col] for col in cols], axis=0)
                own[w] = q
                own[2 + w] = g
                own_t[w] = q.T
                own_t[2 + w] = g.T
            mine = head == head_of_lane + group * heads
            row = jnp.sum(jnp.where(mine, spread, 0.0), axis=0, keepdims=True)
            out[w : w + 1, :] = row * LOG2E
            delta = g.astype(F32) * o.astype(F32)
            row = sum(nt(ones, part) for part in split_bf16(delta, 2))
            out[2 + w : 3 + w, :] = row[0:1]
    spot = lax.rem(lax.broadcasted_iota(jnp.int32, (4, lanes), 1), half).astype(F32)
    own_rows[4:8, :] = spot
    other_rows[4:8, :] = spot
    for i in range(4):
        sib_t[i] = sib[i].T
    kv_out[...] = kv[...]


def is_larger(larger, m, b):
    return jnp.max(larger[2 * m + b : 2 * m + b + 1, :]) > 0.5


def one_run(piece, tokens, half, a, which):
    at = a * tokens + which * half
    if not isinstance(which, int):
        at = pl.multiple_of(at, half)
    rows = piece.shape[0] // 2
    return piece[pl.ds(at, half), :], piece[pl.ds(rows + at, half), :]


def kv_grad_kernel(pair, larger, own, sib, own_t, sib_t, own_rows, sib_rows, piece, *outs):
    tokens = piece.shape[0] // 4
    half = tokens // 2
    lanes = own.shape[1]
    stacks, turned, vectors = (own, sib), (own_t, sib_t), (own_rows, sib_rows)
    first = [one_run(piece, tokens, half, a, 0) for a in range(2)]
    k, v = (jnp.concatenate(x, axis=0) for x in zip(*first))
    jobs = [(k, v, b, 1, None) for b in range(2)]
    for a in range(2):
        for b in range(2):
            if pair == 0 and a == b:
                jobs += [(*one_run(piece, tokens, half, a, w), b, w, (a, w)) for w in range(2)]
            else:
                second = is_larger(larger, 2 * pair + a, b)
                which = jnp.where(second, 1, 0)
                run = one_run(piece, tokens, half, a, which)
                jobs.append((*run, b, which, (a, second)))
    if pair == 0:
        key_row = lax.broadcasted_iota(jnp.int32, (half, lanes), 0)
        query_row = lax.rem(lax.broadcasted_iota(jnp.int32, (half, lanes), 1), half)
        seen = key_row <= query_row

    def products(job):
        k, v, b, which, _ = job
        s = jnp.dot(k, turned[b][which], preferred_element_type=F32)
        return s, jnp.dot(v, turned[b][2 + which], preferred_element_type=F32)

    sums = {(a, w): [] for a in range(2) for w in range(2)}
    ahead = products(jobs[0])
    for i, job in enumerate(jobs):
        (s, dp), ahead = ahead, products(jobs[i + 1]) if i + 1 < len(jobs) else None
        _, _, b, which, place = job
        p = jnp.exp2(s * EXP2_SCALE - vectors[b][pl.ds(which, 1), :])
        if place is not None and isinstance(which, int):
            p = jnp.where(seen, p, 0.0)
        ds = (p * (dp - vectors[b][pl.ds(2 + which, 1), :])).astype(BF16)
        value_term = jnp.dot(p.astype(BF16), stacks[b][2 + which], preferred_element_type=F32)
        key_term = jnp.dot(ds, stacks[b][which], preferred_element_type=F32)
        both = key_term, value_term
        if place is None:
            for a in range(2):
                sums[a, 0].append([x[a * half : (a + 1) * half] for x in both])
        elif isinstance(which, int):
            sums[place].append(both)
        else:
            a, second = place
            sums[a, 0].append([jnp.where(second, 0.0, x) for x in both])
            sums[a, 1].append([jnp.where(second, x, 0.0) for x in both])
    for (a, w), parts in sums.items():
        out = outs[a % len(outs)]
        at = w * half + (a * 2 * tokens if len(outs) == 1 else 0)
        out[at : at + half, :] = (sum(x[0] for x in parts) * SCALE).astype(out.dtype)
        at += tokens
        out[at : at + half, :] = sum(x[1] for x in parts).astype(out.dtype)


def q_grads(b, larger, stack, vectors, pieces):
    tokens = pieces[0].shape[0] // 4
    half = tokens // 2
    rows = 2 * tokens
    grads = [0.0, 0.0]
    columns = vectors[...].T
    spot = columns[:, 4:5]
    for start in range(0, len(pieces), 4):
        some = pieces[start : start + 4]

        def gather(at):
            return jnp.concatenate(
                [x[at + a * tokens : at + a * tokens + half, :] for x in some for a in range(2)],
                axis=0,
            )

        count = 2 * len(some)
        lane = lax.broadcasted_iota(jnp.int32, (1, count * half), 1)
        group = lax.div(lane, half)
        least = [lax.rem(lane, half).astype(F32)] * 2
        for i in range(count):
            m = 2 * start + i
            if m != b:
                sign = jnp.where(is_larger(larger, m, b), 1.0, -1.0) * 2 * tokens
                least[0] = jnp.where(group == i, sign, least[0])
                least[1] = jnp.where(group == i, -sign, least[1])
        runs = [(gather(at), gather(rows + at)) for at in (0, half)]
        for which, run, limit in ((0, 0, least[0]), (1, 0, None), (1, 1, least[1])):
            k, v = runs[run]
            p = jnp.exp2(
                nt(stack[which], k) * EXP2_SCALE - columns[:, which : which + 1]
            )
            if limit is not None:
                p = jnp.where(spot >= limit, p, 0.0)
            delta = columns[:, 2 + which : 3 + which]
            ds = (p * (nt(stack[2 + which], v) - delta)).astype(BF16)
            grads[which] = grads[which] + jnp.dot(ds, k, preferred_element_type=F32)
    return [(x * SCALE).astype(BF16) for x in grads]


def sib_grad_kernel(larger, stack, vectors, *refs):
    pieces, out = refs[:-1], refs[-1]
    out[0], out[1] = q_grads(1, larger, stack, vectors, pieces)


def own_grad_kernel(heads, larger, stack, vectors, other, *refs):
    pieces, (out, held, sems) = refs[:-3], refs[-3:]
    half = out.shape[0] // 2
    c = parity()

    def copies(ref, group):
        return [
            pltpu.make_async_copy(
                ref.at[w, pl.ds(h * half, half), :],
                out.at[pl.ds(w * half, half), columns_of(group * heads + h)],
                sems.at[group_sems + w * heads + h],
            )
            for w in range(2)
            for h in range(heads)
        ]

    group_sems = 0
    first = copies(other, 1 - c)
    group_sems = 2 * heads
    second = copies(held, c)
    for each in first:
        each.start()
    held[0], held[1] = q_grads(0, larger, stack, vectors, pieces)
    for each in second:
        each.start()
    for each in first + second:
        each.wait()


def merge_kv_kernel(*refs):
    parts, out = refs[:-1], refs[-1]
    tokens = parts[0].shape[0]
    cols = columns_of(parity())
    for i, ref in enumerate(parts):
        out[i * tokens : (i + 1) * tokens, :] = ref[:, cols]


def sum_kernel(*refs):
    parts, outs = refs[:-2], refs[-2:]
    size = outs[0].shape[0]
    for a, out in enumerate(outs):
        value = parts[a][...]
        for part in parts[2:]:
            value = value + part[a * size : (a + 1) * size, :].astype(F32)
        out[...] = value


def share_kernel(tp_count, same, same_last, other, other_last, *refs):
    outs, (total,) = refs[:tp_count], refs[tp_count:]
    tokens = same.shape[0] // 2
    share = tokens // tp_count
    c = parity()
    z = lax.axis_index("tp")
    for ref, last, group in ((same, same_last, c), (other, other_last, 1 - c)):
        total[:, columns_of(group)] = ref[...] + last[...].astype(F32)
    for m, out in enumerate(outs):
        start = jnp.bitwise_xor(z, m) * share
        for kind in range(2):
            r = pl.ds(pl.multiple_of(kind * tokens + start, 8), share)
            out[kind] = total[r, :].astype(BF16)


def spread_kernel(tp_count, order, *refs):
    parts, (key_out, value_out) = refs[:tp_count], refs[tp_count:]
    z = lax.axis_index("tp")
    width = parts[0].shape[2]
    for m, part in zip(order, parts):
        cols = pl.ds(pl.multiple_of(jnp.bitwise_xor(z, m) * width, width), width)
        key_out[:, cols] = part[0]
        value_out[:, cols] = part[1]


def swap(x, axis, shift):
    count = lax.axis_size(axis)
    return lax.ppermute(x, axis, [(i, i ^ shift) for i in range(count)])


def on_device(positions, queries, keys, values, attn_output, output_grad, log_sums):
    n = lax.axis_size("ctx")
    tp_count = lax.axis_size("tp")
    tokens = queries.shape[0]
    half = tokens // 2
    heads = log_sums.shape[1] // 2
    lanes = heads * half

    half_piece = ((2 * tokens, HEAD_SIZE), BF16)
    piece = ((4 * tokens, HEAD_SIZE), BF16)
    stack = ((4, lanes, HEAD_SIZE), BF16)
    other, larger = call(
        functools.partial(pack_q_kernel, heads),
        [stack, ((2 * n, HEAD_SIZE), F32)],
        [],
        [pltpu.SMEM(positions.shape, jnp.int32), pltpu.SemaphoreType.DMA((4 * heads + 1,))],
        cost=1.0,
        far=[queries, output_grad, positions],
    )
    pair_keys, pair_values = swap(keys, "ctx", 1), swap(values, "ctx", 1)
    other, pair_keys, pair_values = lax.optimization_barrier((other, pair_keys, pair_values))
    (kv_chip,) = call(merge_kv_kernel, [piece], [keys, pair_keys, values, pair_values])
    sib = swap(other, "ctx", 1)
    turned = ((4, HEAD_SIZE, lanes), BF16)
    vectors = ((8, lanes), F32)
    own_rows, other_rows, own, own_t, sib_t, kv_late = call(
        functools.partial(rows_kernel, heads),
        [vectors, vectors, stack, turned, turned, piece],
        [queries, output_grad, attn_output, log_sums.T, sib, kv_chip],
        cost=1.0,
    )
    sib_rows = swap(other_rows, "ctx", 1)
    late = n // 2 - 1
    pieces = {
        pair: swap(kv_late if pair == late else kv_chip, "ctx", 2 * pair)
        for pair in reversed(range(1, n // 2))
    }
    pieces = [kv_chip] + [pieces[pair] for pair in range(1, n // 2)]

    def kv_grads(pair, after=()):
        if pair in (0, late):
            outs = [(half_piece[0], BF16 if pair else F32)] * 2
        else:
            outs = [piece]
        return call(
            functools.partial(kv_grad_kernel, pair),
            outs,
            [larger, own, sib, own_t, sib_t, own_rows, sib_rows, pieces[pair]],
            cost=0.5,
            after=after,
        )

    partials = {}
    for pair in reversed(range(1, late)):
        partials[pair] = kv_grads(pair, partials[pair + 1] if pair + 1 < late else [])
    partials[late] = kv_grads(late)
    local = kv_grads(0, partials[late][:1])
    received = [swap(partials[pair][0], "ctx", 2 * pair) for pair in range(1, late)]
    last = [swap(x, "ctx", 2 * late + a) for a, x in enumerate(partials[late])]

    sums = ((2 * tokens, HEAD_SIZE), F32)
    sum_same, sum_other = call(sum_kernel, [sums] * 2, [*local, *received])
    sum_pair = swap(sum_other, "ctx", 1)
    (dq_sib,) = call(
        sib_grad_kernel,
        [((2, lanes, HEAD_SIZE), BF16)],
        [larger, sib, sib_rows] + pieces,
        cost=2.5,
        after=[sum_same],
    )
    share = ((2, tokens // tp_count, 2 * HEAD_SIZE), BF16)
    shares = call(
        functools.partial(share_kernel, tp_count),
        [share] * tp_count,
        [sum_same, last[0], sum_pair, last[1]],
        [pltpu.VMEM((2 * tokens, 2 * HEAD_SIZE), F32)],
    )
    dq_sib, *shares = lax.optimization_barrier((dq_sib, *shares))
    dq_other = swap(dq_sib, "ctx", 1)
    (query_grad,) = call(
        functools.partial(own_grad_kernel, heads),
        [(queries.shape, BF16)],
        [larger, own, own_rows, dq_other] + pieces,
        [pltpu.VMEM((2, lanes, HEAD_SIZE), BF16), pltpu.SemaphoreType.DMA((4 * heads,))],
        cost=3.0,
        after=[shares[0]],
        out_spec=HBM,
    )
    order = [0, *range(2, tp_count), 1]
    shares = [shares[0]] + [swap(shares[m], "tp", m) for m in order[1:]]
    final = ((tokens // tp_count, 2 * HEAD_SIZE * tp_count), BF16)
    key_grad, value_grad = call(
        functools.partial(spread_kernel, tp_count, order), [final] * 2, shares, after=[pltpu.with_memory_space_constraint(query_grad, pltpu.HBM)]
    )
    return (query_grad, key_grad, value_grad)


def solution(mesh):
    split = P("ctx", "tp")
    rows = P(("ctx", "tp"), None)
    return jax.shard_map(
        on_device,
        mesh=mesh,
        in_specs=(P(), split, split, split, split, split, split),
        out_specs=(split, rows, rows),
        check_vma=False,
    )
```

```python
import functools
import math

import jax
import jax.numpy as jnp
from jax import lax
from jax.experimental import pallas as pl
from jax.experimental.pallas import tpu as pltpu
from jax.sharding import PartitionSpec as P

HEAD_SIZE = 128
SCALE = 1.0 / math.sqrt(HEAD_SIZE)
EXP2_SCALE = SCALE * math.log2(math.e)
FLOPS_PER_US = 1.1e9
LOG2E = math.log2(math.e)
F32 = jnp.float32
BF16 = jnp.bfloat16
VMEM = pl.BlockSpec(memory_space=pltpu.VMEM)
ANY = pl.BlockSpec(memory_space=pl.ANY)
HBM = pl.BlockSpec(memory_space=pltpu.HBM)
SMEM = pl.BlockSpec(memory_space=pltpu.SMEM)


def call(kernel, outs, ins, scratch=(), smem=0, cost=0.1, far=(), after=(), out_spec=VMEM):
    ins = list(ins) + [pltpu.with_memory_space_constraint(x, pltpu.HBM) for x in far]
    specs = [SMEM] * smem + [VMEM] * (len(ins) - smem - len(far))
    specs += [HBM] * len(far) + [ANY] * len(after)
    moved = sum(x.size * x.dtype.itemsize for x in ins)
    count = len(ins)
    ins = list(ins) + list(after)

    def body(*refs):
        kernel(*refs[:count], *refs[len(ins) :])

    return pl.pallas_call(
        body,
        cost_estimate=pl.CostEstimate(
            flops=int(cost * FLOPS_PER_US), bytes_accessed=moved, transcendentals=0
        ),
        in_specs=specs,
        out_specs=[out_spec] * len(outs),
        out_shape=[jax.ShapeDtypeStruct(shape, dtype) for shape, dtype in outs],
        scratch_shapes=list(scratch),
        compiler_params=pltpu.CompilerParams(vmem_limit_bytes=48 * 2**20),
    )(*ins)


def nt(a, b):
    return lax.dot_general(a, b, (((1,), (1,)), ((), ())), preferred_element_type=F32)


def parity():
    return lax.rem(lax.axis_index("ctx"), 2)


def columns_of(head):
    return pl.ds(pl.multiple_of(head * HEAD_SIZE, HEAD_SIZE), HEAD_SIZE)


def copy_all(pairs, sems):
    copies = [
        pltpu.make_async_copy(src, dst, sems.at[i]) for i, (src, dst) in enumerate(pairs)
    ]
    for each in copies:
        each.start()
    for each in copies:
        each.wait()


def run_starts(pos_ref, tokens, shift):
    ctx = lax.axis_index("ctx")
    return pos_ref[jnp.bitwise_xor(ctx, shift) * tokens]


def pack_q_kernel(q_hbm, g_hbm, pos_hbm, out, larger, pos, sems):
    tokens, width = q_hbm.shape[0], out.shape[2]
    cols = pl.ds(pl.multiple_of((1 - parity()) * width, width), width)
    pairs = [(pos_hbm, pos), (q_hbm.at[:, cols], out.at[0]), (g_hbm.at[:, cols], out.at[1])]
    copy_all(pairs, sems)
    for m in range(larger.shape[0] // 2):
        for b in range(2):
            flag = jnp.where(run_starts(pos, tokens, m) > run_starts(pos, tokens, b), 1.0, 0.0)
            larger[2 * m + b : 2 * m + b + 1, :] = jnp.full((1, HEAD_SIZE), flag, F32)


def split_bf16(x, terms):
    parts = []
    for _ in range(terms):
        part = x.astype(BF16)
        parts.append(part)
        x = x - part.astype(F32)
    return parts


def rows_kernel(heads, q_ref, g_ref, o_ref, log, raw, kv, *refs):
    own_rows, other_rows, own, own_t, sib, sib_t, kv_out = refs
    lanes = own.shape[1]
    half = lanes // heads
    c = parity()
    ones = jnp.ones((8, HEAD_SIZE), BF16)
    groups, tokens = log.shape
    token = lax.broadcasted_iota(jnp.int32, (tokens, lanes), 0)
    lane = lax.broadcasted_iota(jnp.int32, (tokens, lanes), 1)
    head = lax.broadcasted_iota(jnp.int32, (groups, lanes), 0)
    head_of_lane = lax.div(lax.broadcasted_iota(jnp.int32, (groups, lanes), 1), half)
    logs = split_bf16(jnp.clip(log[...], -1e30, 1e30), 3)
    for w in range(2):
        r = slice(w * half, (w + 1) * half)
        place = jnp.where(token == lax.rem(lane, half) + w * half, 1.0, 0.0).astype(BF16)
        spread = sum(jnp.dot(part, place, preferred_element_type=F32) for part in logs)
        for out, group in ((own_rows, c), (other_rows, 1 - c)):
            cols = [columns_of(group * heads + h) for h in range(heads)]
            g, o = (
                jnp.concatenate([ref[r, col] for col in cols], axis=0) for ref in (g_ref, o_ref)
            )
            if out is own_rows:
                q = jnp.concatenate([q_ref[r, col] for col in cols], axis=0)
                own[w] = q
                own[2 + w] = g
                own_t[w] = q.T
                own_t[2 + w] = g.T
            mine = head == head_of_lane + group * heads
            row = jnp.sum(jnp.where(mine, spread, 0.0), axis=0, keepdims=True)
            out[w : w + 1, :] = row * LOG2E
            delta = g.astype(F32) * o.astype(F32)
            row = sum(nt(ones, part) for part in split_bf16(delta, 2))
            out[2 + w : 3 + w, :] = row[0:1]
    spot = lax.rem(lax.broadcasted_iota(jnp.int32, (4, lanes), 1), half).astype(F32)
    own_rows[4:8, :] = spot
    other_rows[4:8, :] = spot
    for kind in range(2):
        for w in range(2):
            r = slice(w * half, (w + 1) * half)
            cols = [slice(h * HEAD_SIZE, (h + 1) * HEAD_SIZE) for h in range(heads)]
            x = jnp.concatenate([raw[kind, r, col] for col in cols], axis=0)
            sib[2 * kind + w] = x
            sib_t[2 * kind + w] = x.T
    kv_out[...] = kv[...]


def is_larger(larger, m, b):
    return jnp.max(larger[2 * m + b : 2 * m + b + 1, :]) > 0.5


def one_run(piece, tokens, half, a, which):
    at = a * tokens + which * half
    if not isinstance(which, int):
        at = pl.multiple_of(at, half)
    rows = piece.shape[0] // 2
    return piece[pl.ds(at, half), :], piece[pl.ds(rows + at, half), :]


def kv_grad_kernel(pair, larger, own, sib, own_t, sib_t, own_rows, sib_rows, piece, *outs):
    tokens = piece.shape[0] // 4
    half = tokens // 2
    lanes = own.shape[1]
    stacks, turned, vectors = (own, sib), (own_t, sib_t), (own_rows, sib_rows)
    first = [one_run(piece, tokens, half, a, 0) for a in range(2)]
    k, v = (jnp.concatenate(x, axis=0) for x in zip(*first))
    jobs = [(k, v, b, 1, None) for b in range(2)]
    for a in range(2):
        for b in range(2):
            if pair == 0 and a == b:
                jobs += [(*one_run(piece, tokens, half, a, w), b, w, (a, w)) for w in range(2)]
            else:
                second = is_larger(larger, 2 * pair + a, b)
                which = jnp.where(second, 1, 0)
                run = one_run(piece, tokens, half, a, which)
                jobs.append((*run, b, which, (a, second)))
    if pair == 0:
        key_row = lax.broadcasted_iota(jnp.int32, (half, lanes), 0)
        query_row = lax.rem(lax.broadcasted_iota(jnp.int32, (half, lanes), 1), half)
        seen = key_row <= query_row

    def products(job):
        k, v, b, which, _ = job
        s = jnp.dot(k, turned[b][which], preferred_element_type=F32)
        return s, jnp.dot(v, turned[b][2 + which], preferred_element_type=F32)

    sums = {(a, w): [] for a in range(2) for w in range(2)}
    ahead = products(jobs[0])
    for i, job in enumerate(jobs):
        (s, dp), ahead = ahead, products(jobs[i + 1]) if i + 1 < len(jobs) else None
        _, _, b, which, place = job
        p = jnp.exp2(s * EXP2_SCALE - vectors[b][pl.ds(which, 1), :])
        if place is not None and isinstance(which, int):
            p = jnp.where(seen, p, 0.0)
        ds = (p * (dp - vectors[b][pl.ds(2 + which, 1), :])).astype(BF16)
        value_term = jnp.dot(p.astype(BF16), stacks[b][2 + which], preferred_element_type=F32)
        key_term = jnp.dot(ds, stacks[b][which], preferred_element_type=F32)
        both = key_term, value_term
        if place is None:
            for a in range(2):
                sums[a, 0].append([x[a * half : (a + 1) * half] for x in both])
        elif isinstance(which, int):
            sums[place].append(both)
        else:
            a, second = place
            sums[a, 0].append([jnp.where(second, 0.0, x) for x in both])
            sums[a, 1].append([jnp.where(second, x, 0.0) for x in both])
    for (a, w), parts in sums.items():
        out = outs[a % len(outs)]
        at = w * half + (a * 2 * tokens if len(outs) == 1 else 0)
        out[at : at + half, :] = (sum(x[0] for x in parts) * SCALE).astype(out.dtype)
        at += tokens
        out[at : at + half, :] = sum(x[1] for x in parts).astype(out.dtype)


def q_grads(b, larger, stack, vectors, pieces):
    tokens = pieces[0].shape[0] // 4
    half = tokens // 2
    rows = 2 * tokens
    grads = [0.0, 0.0]
    columns = vectors[...].T
    spot = columns[:, 4:5]
    for start in range(0, len(pieces), 4):
        some = pieces[start : start + 4]

        def gather(at):
            return jnp.concatenate(
                [x[at + a * tokens : at + a * tokens + half, :] for x in some for a in range(2)],
                axis=0,
            )

        count = 2 * len(some)
        lane = lax.broadcasted_iota(jnp.int32, (1, count * half), 1)
        group = lax.div(lane, half)
        least = [lax.rem(lane, half).astype(F32)] * 2
        for i in range(count):
            m = 2 * start + i
            if m != b:
                sign = jnp.where(is_larger(larger, m, b), 1.0, -1.0) * 2 * tokens
                least[0] = jnp.where(group == i, sign, least[0])
                least[1] = jnp.where(group == i, -sign, least[1])
        runs = [(gather(at), gather(rows + at)) for at in (0, half)]
        for which, run, limit in ((0, 0, least[0]), (1, 0, None), (1, 1, least[1])):
            k, v = runs[run]
            p = jnp.exp2(
                nt(stack[which], k) * EXP2_SCALE - columns[:, which : which + 1]
            )
            if limit is not None:
                p = jnp.where(spot >= limit, p, 0.0)
            delta = columns[:, 2 + which : 3 + which]
            ds = (p * (nt(stack[2 + which], v) - delta)).astype(BF16)
            grads[which] = grads[which] + jnp.dot(ds, k, preferred_element_type=F32)
    return [(x * SCALE).astype(BF16) for x in grads]


def sib_grad_kernel(larger, stack, vectors, *refs):
    pieces, out = refs[:-1], refs[-1]
    out[0], out[1] = q_grads(1, larger, stack, vectors, pieces)


def own_grad_kernel(heads, larger, stack, vectors, other, *refs):
    pieces, (out, held, sems) = refs[:-3], refs[-3:]
    half = out.shape[0] // 2
    c = parity()

    def copies(ref, group):
        return [
            pltpu.make_async_copy(
                ref.at[w, pl.ds(h * half, half), :],
                out.at[pl.ds(w * half, half), columns_of(group * heads + h)],
                sems.at[group_sems + w * heads + h],
            )
            for w in range(2)
            for h in range(heads)
        ]

    group_sems = 0
    first = copies(other, 1 - c)
    group_sems = 2 * heads
    second = copies(held, c)
    for each in first:
        each.start()
    held[0], held[1] = q_grads(0, larger, stack, vectors, pieces)
    for each in second:
        each.start()
    for each in first + second:
        each.wait()


def merge_kv_kernel(*refs):
    parts, out = refs[:-1], refs[-1]
    tokens = parts[0].shape[0]
    cols = columns_of(parity())
    for i, ref in enumerate(parts):
        out[i * tokens : (i + 1) * tokens, :] = ref[:, cols]


def sum_kernel(*refs):
    parts, outs = refs[:-2], refs[-2:]
    size = outs[0].shape[0]
    for a, out in enumerate(outs):
        value = parts[a][...]
        for part in parts[2:]:
            value = value + part[a * size : (a + 1) * size, :].astype(F32)
        out[...] = value


def share_kernel(tp_count, same, same_last, other, other_last, *refs):
    outs, (total,) = refs[:tp_count], refs[tp_count:]
    tokens = same.shape[0] // 2
    share = tokens // tp_count
    c = parity()
    z = lax.axis_index("tp")
    for ref, last, group in ((same, same_last, c), (other, other_last, 1 - c)):
        total[:, columns_of(group)] = ref[...] + last[...].astype(F32)
    for m, out in enumerate(outs):
        start = jnp.bitwise_xor(z, m) * share
        for kind in range(2):
            r = pl.ds(pl.multiple_of(kind * tokens + start, 8), share)
            out[kind] = total[r, :].astype(BF16)


def spread_kernel(tp_count, order, *refs):
    parts, (key_out, value_out) = refs[:tp_count], refs[tp_count:]
    z = lax.axis_index("tp")
    width = parts[0].shape[2]
    for m, part in zip(order, parts):
        cols = pl.ds(pl.multiple_of(jnp.bitwise_xor(z, m) * width, width), width)
        key_out[:, cols] = part[0]
        value_out[:, cols] = part[1]


def swap(x, axis, shift):
    count = lax.axis_size(axis)
    return lax.ppermute(x, axis, [(i, i ^ shift) for i in range(count)])


def on_device(positions, queries, keys, values, attn_output, output_grad, log_sums):
    n = lax.axis_size("ctx")
    tp_count = lax.axis_size("tp")
    tokens = queries.shape[0]
    half = tokens // 2
    heads = log_sums.shape[1] // 2
    lanes = heads * half

    half_piece = ((2 * tokens, HEAD_SIZE), BF16)
    piece = ((4 * tokens, HEAD_SIZE), BF16)
    stack = ((4, lanes, HEAD_SIZE), BF16)
    other, larger = call(
        pack_q_kernel,
        [((2, tokens, heads * HEAD_SIZE), BF16), ((2 * n, HEAD_SIZE), F32)],
        [],
        [pltpu.SMEM(positions.shape, jnp.int32), pltpu.SemaphoreType.DMA((3,))],
        cost=1.0,
        far=[queries, output_grad, positions],
    )
    pair_keys, pair_values = swap(keys, "ctx", 1), swap(values, "ctx", 1)
    other, pair_keys, pair_values = lax.optimization_barrier((other, pair_keys, pair_values))
    (kv_chip,) = call(merge_kv_kernel, [piece], [keys, pair_keys, values, pair_values])
    raw = swap(other, "ctx", 1)
    turned = ((4, HEAD_SIZE, lanes), BF16)
    vectors = ((8, lanes), F32)
    own_rows, other_rows, own, own_t, sib, sib_t, kv_late = call(
        functools.partial(rows_kernel, heads),
        [vectors, vectors, stack, turned, stack, turned, piece],
        [queries, output_grad, attn_output, log_sums.T, raw, kv_chip],
        cost=1.0,
    )
    sib_rows = swap(other_rows, "ctx", 1)
    late = n // 2 - 1
    pieces = {
        pair: swap(kv_late if pair == late else kv_chip, "ctx", 2 * pair)
        for pair in reversed(range(1, n // 2))
    }
    pieces = [kv_chip] + [pieces[pair] for pair in range(1, n // 2)]

    def kv_grads(pair, after=()):
        if pair in (0, late):
            outs = [(half_piece[0], BF16 if pair else F32)] * 2
        else:
            outs = [piece]
        return call(
            functools.partial(kv_grad_kernel, pair),
            outs,
            [larger, own, sib, own_t, sib_t, own_rows, sib_rows, pieces[pair]],
            cost=0.5,
            after=after,
        )

    partials = {}
    for pair in reversed(range(1, late)):
        partials[pair] = kv_grads(pair, partials[pair + 1] if pair + 1 < late else [])
    partials[late] = kv_grads(late)
    local = kv_grads(0, partials[late][:1])
    received = [swap(partials[pair][0], "ctx", 2 * pair) for pair in range(1, late)]
    last = [swap(x, "ctx", 2 * late + a) for a, x in enumerate(partials[late])]

    sums = ((2 * tokens, HEAD_SIZE), F32)
    sum_same, sum_other = call(sum_kernel, [sums] * 2, [*local, *received])
    sum_pair = swap(sum_other, "ctx", 1)
    (dq_sib,) = call(
        sib_grad_kernel,
        [((2, lanes, HEAD_SIZE), BF16)],
        [larger, sib, sib_rows] + pieces,
        cost=2.5,
        after=[sum_same],
    )
    share = ((2, tokens // tp_count, 2 * HEAD_SIZE), BF16)
    shares = call(
        functools.partial(share_kernel, tp_count),
        [share] * tp_count,
        [sum_same, last[0], sum_pair, last[1]],
        [pltpu.VMEM((2 * tokens, 2 * HEAD_SIZE), F32)],
    )
    dq_sib, *shares = lax.optimization_barrier((dq_sib, *shares))
    dq_other = swap(dq_sib, "ctx", 1)
    (query_grad,) = call(
        functools.partial(own_grad_kernel, heads),
        [(queries.shape, BF16)],
        [larger, own, own_rows, dq_other] + pieces,
        [pltpu.VMEM((2, lanes, HEAD_SIZE), BF16), pltpu.SemaphoreType.DMA((4 * heads,))],
        cost=3.0,
        after=[shares[0]],
        out_spec=HBM,
    )
    order = [0, *range(2, tp_count), 1]
    shares = [shares[0]] + [swap(shares[m], "tp", m) for m in order[1:]]
    final = ((tokens // tp_count, 2 * HEAD_SIZE * tp_count), BF16)
    key_grad, value_grad = call(
        functools.partial(spread_kernel, tp_count, order), [final] * 2, shares, after=[pltpu.with_memory_space_constraint(query_grad, pltpu.HBM)]
    )
    return (query_grad, key_grad, value_grad)


def solution(mesh):
    split = P("ctx", "tp")
    rows = P(("ctx", "tp"), None)
    return jax.shard_map(
        on_device,
        mesh=mesh,
        in_specs=(P(), split, split, split, split, split, split),
        out_specs=(split, rows, rows),
        check_vma=False,
    )
```

```python
import functools
import math

import jax
import jax.numpy as jnp
from jax import lax
from jax.experimental import pallas as pl
from jax.experimental.pallas import tpu as pltpu
from jax.sharding import PartitionSpec as P

HEAD_SIZE = 128
SCALE = 1.0 / math.sqrt(HEAD_SIZE)
EXP2_SCALE = SCALE * math.log2(math.e)
FLOPS_PER_US = 1.1e9
LOG2E = math.log2(math.e)
F32 = jnp.float32
BF16 = jnp.bfloat16
VMEM = pl.BlockSpec(memory_space=pltpu.VMEM)
ANY = pl.BlockSpec(memory_space=pl.ANY)
HBM = pl.BlockSpec(memory_space=pltpu.HBM)
SMEM = pl.BlockSpec(memory_space=pltpu.SMEM)


def call(kernel, outs, ins, scratch=(), smem=0, cost=0.1, far=(), after=(), out_spec=VMEM):
    ins = list(ins) + [pltpu.with_memory_space_constraint(x, pltpu.HBM) for x in far]
    specs = [SMEM] * smem + [VMEM] * (len(ins) - smem - len(far))
    specs += [HBM] * len(far) + [ANY] * len(after)
    moved = sum(x.size * x.dtype.itemsize for x in ins)
    count = len(ins)
    ins = list(ins) + list(after)

    def body(*refs):
        kernel(*refs[:count], *refs[len(ins) :])

    return pl.pallas_call(
        body,
        cost_estimate=pl.CostEstimate(
            flops=int(cost * FLOPS_PER_US), bytes_accessed=moved, transcendentals=0
        ),
        in_specs=specs,
        out_specs=[out_spec] * len(outs),
        out_shape=[jax.ShapeDtypeStruct(shape, dtype) for shape, dtype in outs],
        scratch_shapes=list(scratch),
        compiler_params=pltpu.CompilerParams(vmem_limit_bytes=48 * 2**20),
    )(*ins)


def nt(a, b):
    return lax.dot_general(a, b, (((1,), (1,)), ((), ())), preferred_element_type=F32)


def parity():
    return lax.rem(lax.axis_index("ctx"), 2)


def columns_of(head):
    return pl.ds(pl.multiple_of(head * HEAD_SIZE, HEAD_SIZE), HEAD_SIZE)


def copy_all(pairs, sems):
    copies = [
        pltpu.make_async_copy(src, dst, sems.at[i]) for i, (src, dst) in enumerate(pairs)
    ]
    for each in copies:
        each.start()
    for each in copies:
        each.wait()


def run_starts(pos_ref, tokens, shift):
    ctx = lax.axis_index("ctx")
    return pos_ref[jnp.bitwise_xor(ctx, shift) * tokens]


def pack_q_kernel(q_hbm, g_hbm, pos_hbm, out, larger, pos, sems):
    tokens, width = q_hbm.shape[0], out.shape[2]
    cols = pl.ds(pl.multiple_of((1 - parity()) * width, width), width)
    pairs = [(pos_hbm, pos), (q_hbm.at[:, cols], out.at[0]), (g_hbm.at[:, cols], out.at[1])]
    copy_all(pairs, sems)
    for m in range(larger.shape[0] // 2):
        for b in range(2):
            flag = jnp.where(run_starts(pos, tokens, m) > run_starts(pos, tokens, b), 1.0, 0.0)
            larger[2 * m + b : 2 * m + b + 1, :] = jnp.full((1, HEAD_SIZE), flag, F32)


def split_bf16(x, terms):
    parts = []
    for _ in range(terms):
        part = x.astype(BF16)
        parts.append(part)
        x = x - part.astype(F32)
    return parts


def rows_kernel(heads, q_ref, g_ref, o_ref, log, raw, kv, *refs):
    own_rows, other_rows, own, own_t, sib, sib_t, kv_out = refs
    lanes = own.shape[1]
    half = lanes // heads
    c = parity()
    ones = jnp.ones((8, HEAD_SIZE), BF16)
    groups, tokens = log.shape
    token = lax.broadcasted_iota(jnp.int32, (tokens, lanes), 0)
    lane = lax.broadcasted_iota(jnp.int32, (tokens, lanes), 1)
    head = lax.broadcasted_iota(jnp.int32, (groups, lanes), 0)
    head_of_lane = lax.div(lax.broadcasted_iota(jnp.int32, (groups, lanes), 1), half)
    logs = split_bf16(jnp.clip(log[...], -1e30, 1e30), 3)
    for w in range(2):
        r = slice(w * half, (w + 1) * half)
        place = jnp.where(token == lax.rem(lane, half) + w * half, 1.0, 0.0).astype(BF16)
        spread = sum(jnp.dot(part, place, preferred_element_type=F32) for part in logs)
        for out, group in ((own_rows, c), (other_rows, 1 - c)):
            cols = [columns_of(group * heads + h) for h in range(heads)]
            g, o = (
                jnp.concatenate([ref[r, col] for col in cols], axis=0) for ref in (g_ref, o_ref)
            )
            if out is own_rows:
                q = jnp.concatenate([q_ref[r, col] for col in cols], axis=0)
                own[w] = q
                own[2 + w] = g
                own_t[w] = q.T
                own_t[2 + w] = g.T
            mine = head == head_of_lane + group * heads
            row = jnp.sum(jnp.where(mine, spread, 0.0), axis=0, keepdims=True)
            out[w : w + 1, :] = row * LOG2E
            delta = g.astype(F32) * o.astype(F32)
            row = sum(nt(ones, part) for part in split_bf16(delta, 2))
            out[2 + w : 3 + w, :] = row[0:1]
    spot = lax.rem(lax.broadcasted_iota(jnp.int32, (4, lanes), 1), half).astype(F32)
    own_rows[4:8, :] = spot
    other_rows[4:8, :] = spot
    for kind in range(2):
        for w in range(2):
            r = slice(w * half, (w + 1) * half)
            cols = [slice(h * HEAD_SIZE, (h + 1) * HEAD_SIZE) for h in range(heads)]
            x = jnp.concatenate([raw[kind, r, col] for col in cols], axis=0)
            sib[2 * kind + w] = x
            sib_t[2 * kind + w] = x.T
    kv_out[...] = kv[...]


def is_larger(larger, m, b):
    return jnp.max(larger[2 * m + b : 2 * m + b + 1, :]) > 0.5


def one_run(piece, tokens, half, a, which):
    at = a * tokens + which * half
    if not isinstance(which, int):
        at = pl.multiple_of(at, half)
    rows = piece.shape[0] // 2
    return piece[pl.ds(at, half), :], piece[pl.ds(rows + at, half), :]


def kv_grad_kernel(pair, larger, own, sib, own_t, sib_t, own_rows, sib_rows, piece, *outs):
    tokens = piece.shape[0] // 4
    half = tokens // 2
    lanes = own.shape[1]
    stacks, turned, vectors = (own, sib), (own_t, sib_t), (own_rows, sib_rows)
    first = [one_run(piece, tokens, half, a, 0) for a in range(2)]
    k, v = (jnp.concatenate(x, axis=0) for x in zip(*first))
    jobs = [(k, v, b, 1, None) for b in range(2)]
    for a in range(2):
        for b in range(2):
            if pair == 0 and a == b:
                jobs += [(*one_run(piece, tokens, half, a, w), b, w, (a, w)) for w in range(2)]
            else:
                second = is_larger(larger, 2 * pair + a, b)
                which = jnp.where(second, 1, 0)
                run = one_run(piece, tokens, half, a, which)
                jobs.append((*run, b, which, (a, second)))
    if pair == 0:
        key_row = lax.broadcasted_iota(jnp.int32, (half, lanes), 0)
        query_row = lax.rem(lax.broadcasted_iota(jnp.int32, (half, lanes), 1), half)
        seen = key_row <= query_row

    def products(job):
        k, v, b, which, _ = job
        s = jnp.dot(k, turned[b][which], preferred_element_type=F32)
        return s, jnp.dot(v, turned[b][2 + which], preferred_element_type=F32)

    sums = {(a, w): [] for a in range(2) for w in range(2)}
    ahead = products(jobs[0])
    for i, job in enumerate(jobs):
        (s, dp), ahead = ahead, products(jobs[i + 1]) if i + 1 < len(jobs) else None
        _, _, b, which, place = job
        p = jnp.exp2(s * EXP2_SCALE - vectors[b][pl.ds(which, 1), :])
        if place is not None and isinstance(which, int):
            p = jnp.where(seen, p, 0.0)
        ds = (p * (dp - vectors[b][pl.ds(2 + which, 1), :])).astype(BF16)
        value_term = jnp.dot(p.astype(BF16), stacks[b][2 + which], preferred_element_type=F32)
        key_term = jnp.dot(ds, stacks[b][which], preferred_element_type=F32)
        both = key_term, value_term
        if place is None:
            for a in range(2):
                sums[a, 0].append([x[a * half : (a + 1) * half] for x in both])
        elif isinstance(which, int):
            sums[place].append(both)
        else:
            a, second = place
            sums[a, 0].append([jnp.where(second, 0.0, x) for x in both])
            sums[a, 1].append([jnp.where(second, x, 0.0) for x in both])
    for (a, w), parts in sums.items():
        out = outs[a % len(outs)]
        at = w * half + (a * 2 * tokens if len(outs) == 1 else 0)
        out[at : at + half, :] = (sum(x[0] for x in parts) * SCALE).astype(out.dtype)
        at += tokens
        out[at : at + half, :] = sum(x[1] for x in parts).astype(out.dtype)


def q_grads(b, larger, stack, vectors, pieces):
    tokens = pieces[0].shape[0] // 4
    half = tokens // 2
    rows = 2 * tokens
    jobs = {0: [], 1: []}
    columns = vectors[...].T
    spot = columns[:, 4:5]
    for start in range(0, len(pieces), 4):
        some = pieces[start : start + 4]

        def gather(at):
            return jnp.concatenate(
                [x[at + a * tokens : at + a * tokens + half, :] for x in some for a in range(2)],
                axis=0,
            )

        count = 2 * len(some)
        lane = lax.broadcasted_iota(jnp.int32, (1, count * half), 1)
        group = lax.div(lane, half)
        least = [lax.rem(lane, half).astype(F32)] * 2
        for i in range(count):
            m = 2 * start + i
            if m != b:
                sign = jnp.where(is_larger(larger, m, b), 1.0, -1.0) * 2 * tokens
                least[0] = jnp.where(group == i, sign, least[0])
                least[1] = jnp.where(group == i, -sign, least[1])
        runs = [(gather(at), gather(rows + at)) for at in (0, half)]
        jobs[1] += [(1, runs[0], None), (1, runs[1], least[1])]
        jobs[0].append((0, runs[0], least[0]))
    listed = jobs[1] + jobs[0]

    def products(job):
        which, (k, v), _ = job
        return nt(stack[which], k), nt(stack[2 + which], v)

    grad = 0.0
    ahead = products(listed[0])
    for i, (which, (k, _), limit) in enumerate(listed):
        (s, dp), ahead = ahead, products(listed[i + 1]) if i + 1 < len(listed) else None
        p = jnp.exp2(s * EXP2_SCALE - columns[:, which : which + 1])
        if limit is not None:
            p = jnp.where(spot >= limit, p, 0.0)
        ds = (p * (dp - columns[:, 2 + which : 3 + which])).astype(BF16)
        grad = grad + jnp.dot(ds, k, preferred_element_type=F32)
        if i + 1 == len(listed) or listed[i + 1][0] != which:
            yield which, (grad * SCALE).astype(BF16)
            grad = 0.0


def sib_grad_kernel(larger, stack, vectors, *refs):
    pieces, out = refs[:-1], refs[-1]
    for which, grad in q_grads(1, larger, stack, vectors, pieces):
        out[which] = grad


def own_grad_kernel(heads, larger, stack, vectors, other, *refs):
    pieces, (out, held, sems) = refs[:-3], refs[-3:]
    half = out.shape[0] // 2
    c = parity()

    def copies(ref, group):
        return [
            pltpu.make_async_copy(
                ref.at[w, pl.ds(h * half, half), :],
                out.at[pl.ds(w * half, half), columns_of(group * heads + h)],
                sems.at[group_sems + w * heads + h],
            )
            for w in range(2)
            for h in range(heads)
        ]

    group_sems = 0
    first = copies(other, 1 - c)
    group_sems = 2 * heads
    second = copies(held, c)
    for each in first:
        each.start()
    for which, grad in q_grads(0, larger, stack, vectors, pieces):
        held[which] = grad
        for each in second[which * heads : (which + 1) * heads]:
            each.start()
    for each in first + second:
        each.wait()


def merge_kv_kernel(*refs):
    parts, out = refs[:-1], refs[-1]
    tokens = parts[0].shape[0]
    cols = columns_of(parity())
    for i, ref in enumerate(parts):
        out[i * tokens : (i + 1) * tokens, :] = ref[:, cols]


def sum_kernel(*refs):
    parts, outs = refs[:-2], refs[-2:]
    size = outs[0].shape[0]
    for a, out in enumerate(outs):
        value = parts[a][...]
        for part in parts[2:]:
            value = value + part[a * size : (a + 1) * size, :].astype(F32)
        out[...] = value


def share_kernel(tp_count, same, same_last, other, other_last, *refs):
    outs, (total,) = refs[:tp_count], refs[tp_count:]
    tokens = same.shape[0] // 2
    share = tokens // tp_count
    c = parity()
    z = lax.axis_index("tp")
    for ref, last, group in ((same, same_last, c), (other, other_last, 1 - c)):
        total[:, columns_of(group)] = ref[...] + last[...].astype(F32)
    for m, out in enumerate(outs):
        start = jnp.bitwise_xor(z, m) * share
        for kind in range(2):
            r = pl.ds(pl.multiple_of(kind * tokens + start, 8), share)
            out[kind] = total[r, :].astype(BF16)


def spread_kernel(tp_count, order, *refs):
    parts, (key_out, value_out) = refs[:tp_count], refs[tp_count:]
    z = lax.axis_index("tp")
    width = parts[0].shape[2]
    for m, part in zip(order, parts):
        cols = pl.ds(pl.multiple_of(jnp.bitwise_xor(z, m) * width, width), width)
        key_out[:, cols] = part[0]
        value_out[:, cols] = part[1]


def swap(x, axis, shift):
    count = lax.axis_size(axis)
    return lax.ppermute(x, axis, [(i, i ^ shift) for i in range(count)])


def on_device(positions, queries, keys, values, attn_output, output_grad, log_sums):
    n = lax.axis_size("ctx")
    tp_count = lax.axis_size("tp")
    tokens = queries.shape[0]
    half = tokens // 2
    heads = log_sums.shape[1] // 2
    lanes = heads * half

    half_piece = ((2 * tokens, HEAD_SIZE), BF16)
    piece = ((4 * tokens, HEAD_SIZE), BF16)
    stack = ((4, lanes, HEAD_SIZE), BF16)
    other, larger = call(
        pack_q_kernel,
        [((2, tokens, heads * HEAD_SIZE), BF16), ((2 * n, HEAD_SIZE), F32)],
        [],
        [pltpu.SMEM(positions.shape, jnp.int32), pltpu.SemaphoreType.DMA((3,))],
        cost=1.0,
        far=[queries, output_grad, positions],
    )
    pair_keys, pair_values = swap(keys, "ctx", 1), swap(values, "ctx", 1)
    other, pair_keys, pair_values = lax.optimization_barrier((other, pair_keys, pair_values))
    (kv_chip,) = call(merge_kv_kernel, [piece], [keys, pair_keys, values, pair_values])
    raw = swap(other, "ctx", 1)
    turned = ((4, HEAD_SIZE, lanes), BF16)
    vectors = ((8, lanes), F32)
    own_rows, other_rows, own, own_t, sib, sib_t, kv_late = call(
        functools.partial(rows_kernel, heads),
        [vectors, vectors, stack, turned, stack, turned, piece],
        [queries, output_grad, attn_output, log_sums.T, raw, kv_chip],
        cost=1.0,
    )
    sib_rows = swap(other_rows, "ctx", 1)
    late = n // 2 - 1
    pieces = {
        pair: swap(kv_late if pair == late else kv_chip, "ctx", 2 * pair)
        for pair in reversed(range(1, n // 2))
    }
    pieces = [kv_chip] + [pieces[pair] for pair in range(1, n // 2)]

    def kv_grads(pair, after=()):
        if pair in (0, late):
            outs = [(half_piece[0], BF16 if pair else F32)] * 2
        else:
            outs = [piece]
        return call(
            functools.partial(kv_grad_kernel, pair),
            outs,
            [larger, own, sib, own_t, sib_t, own_rows, sib_rows, pieces[pair]],
            cost=0.5,
            after=after,
        )

    partials = {}
    for pair in reversed(range(1, late)):
        partials[pair] = kv_grads(pair, partials[pair + 1] if pair + 1 < late else [])
    partials[late] = kv_grads(late)
    local = kv_grads(0, partials[late][:1])
    received = [swap(partials[pair][0], "ctx", 2 * pair) for pair in range(1, late)]
    last = [swap(x, "ctx", 2 * late + a) for a, x in enumerate(partials[late])]

    sums = ((2 * tokens, HEAD_SIZE), F32)
    sum_same, sum_other = call(sum_kernel, [sums] * 2, [*local, *received])
    sum_pair = swap(sum_other, "ctx", 1)
    (dq_sib,) = call(
        sib_grad_kernel,
        [((2, lanes, HEAD_SIZE), BF16)],
        [larger, sib, sib_rows] + pieces,
        cost=2.5,
        after=[sum_same],
    )
    share = ((2, tokens // tp_count, 2 * HEAD_SIZE), BF16)
    shares = call(
        functools.partial(share_kernel, tp_count),
        [share] * tp_count,
        [sum_same, last[0], sum_pair, last[1]],
        [pltpu.VMEM((2 * tokens, 2 * HEAD_SIZE), F32)],
    )
    dq_sib, *shares = lax.optimization_barrier((dq_sib, *shares))
    dq_other = swap(dq_sib, "ctx", 1)
    (query_grad,) = call(
        functools.partial(own_grad_kernel, heads),
        [(queries.shape, BF16)],
        [larger, own, own_rows, dq_other] + pieces,
        [pltpu.VMEM((2, lanes, HEAD_SIZE), BF16), pltpu.SemaphoreType.DMA((4 * heads,))],
        cost=3.0,
        after=[shares[0]],
        out_spec=HBM,
    )
    order = [0, *range(2, tp_count), 1]
    shares = [shares[0]] + [swap(shares[m], "tp", m) for m in order[1:]]
    final = ((tokens // tp_count, 2 * HEAD_SIZE * tp_count), BF16)
    key_grad, value_grad = call(
        functools.partial(spread_kernel, tp_count, order), [final] * 2, shares, after=[pltpu.with_memory_space_constraint(query_grad, pltpu.HBM)]
    )
    return (query_grad, key_grad, value_grad)


def solution(mesh):
    split = P("ctx", "tp")
    rows = P(("ctx", "tp"), None)
    return jax.shard_map(
        on_device,
        mesh=mesh,
        in_specs=(P(), split, split, split, split, split, split),
        out_specs=(split, rows, rows),
        check_vma=False,
    )
```

```python
import functools
import math

import jax
import jax.numpy as jnp
from jax import lax
from jax.experimental import pallas as pl
from jax.experimental.pallas import tpu as pltpu
from jax.sharding import PartitionSpec as P

HEAD_SIZE = 128
SCALE = 1.0 / math.sqrt(HEAD_SIZE)
EXP2_SCALE = SCALE * math.log2(math.e)
FLOPS_PER_US = 1.1e9
LOG2E = math.log2(math.e)
F32 = jnp.float32
BF16 = jnp.bfloat16
VMEM = pl.BlockSpec(memory_space=pltpu.VMEM)
ANY = pl.BlockSpec(memory_space=pl.ANY)
HBM = pl.BlockSpec(memory_space=pltpu.HBM)
SMEM = pl.BlockSpec(memory_space=pltpu.SMEM)


def call(kernel, outs, ins, scratch=(), smem=0, cost=0.1, far=(), after=(), out_spec=VMEM):
    ins = list(ins) + [pltpu.with_memory_space_constraint(x, pltpu.HBM) for x in far]
    specs = [SMEM] * smem + [VMEM] * (len(ins) - smem - len(far))
    specs += [HBM] * len(far) + [ANY] * len(after)
    moved = sum(x.size * x.dtype.itemsize for x in ins)
    count = len(ins)
    ins = list(ins) + list(after)

    def body(*refs):
        kernel(*refs[:count], *refs[len(ins) :])

    return pl.pallas_call(
        body,
        cost_estimate=pl.CostEstimate(
            flops=int(cost * FLOPS_PER_US), bytes_accessed=moved, transcendentals=0
        ),
        in_specs=specs,
        out_specs=[out_spec] * len(outs),
        out_shape=[jax.ShapeDtypeStruct(shape, dtype) for shape, dtype in outs],
        scratch_shapes=list(scratch),
        compiler_params=pltpu.CompilerParams(vmem_limit_bytes=48 * 2**20),
    )(*ins)


def nt(a, b):
    return lax.dot_general(a, b, (((1,), (1,)), ((), ())), preferred_element_type=F32)


def parity():
    return lax.rem(lax.axis_index("ctx"), 2)


def columns_of(head):
    return pl.ds(pl.multiple_of(head * HEAD_SIZE, HEAD_SIZE), HEAD_SIZE)


def copy_all(pairs, sems):
    copies = [
        pltpu.make_async_copy(src, dst, sems.at[i]) for i, (src, dst) in enumerate(pairs)
    ]
    for each in copies:
        each.start()
    for each in copies:
        each.wait()


def run_starts(pos_ref, tokens, shift):
    ctx = lax.axis_index("ctx")
    return pos_ref[jnp.bitwise_xor(ctx, shift) * tokens]


def pack_q_kernel(q_hbm, g_hbm, pos_hbm, out, larger, pos, sems):
    tokens, width = q_hbm.shape[0], out.shape[2]
    cols = pl.ds(pl.multiple_of((1 - parity()) * width, width), width)
    pairs = [(pos_hbm, pos), (q_hbm.at[:, cols], out.at[0]), (g_hbm.at[:, cols], out.at[1])]
    copy_all(pairs, sems)
    for m in range(larger.shape[0] // 2):
        for b in range(2):
            flag = jnp.where(run_starts(pos, tokens, m) > run_starts(pos, tokens, b), 1.0, 0.0)
            larger[2 * m + b : 2 * m + b + 1, :] = jnp.full((1, HEAD_SIZE), flag, F32)


def split_bf16(x, terms):
    parts = []
    for _ in range(terms):
        part = x.astype(BF16)
        parts.append(part)
        x = x - part.astype(F32)
    return parts


def rows_kernel(heads, q_ref, g_ref, o_ref, log, raw, kv, *refs):
    own_rows, other_rows, own, own_t, sib, sib_t, kv_out = refs
    lanes = own.shape[1]
    half = lanes // heads
    c = parity()
    ones = jnp.ones((8, HEAD_SIZE), BF16)
    groups, tokens = log.shape
    token = lax.broadcasted_iota(jnp.int32, (tokens, lanes), 0)
    lane = lax.broadcasted_iota(jnp.int32, (tokens, lanes), 1)
    head = lax.broadcasted_iota(jnp.int32, (groups, lanes), 0)
    head_of_lane = lax.div(lax.broadcasted_iota(jnp.int32, (groups, lanes), 1), half)
    logs = split_bf16(jnp.clip(log[...], -1e30, 1e30), 3)
    for w in range(2):
        r = slice(w * half, (w + 1) * half)
        place = jnp.where(token == lax.rem(lane, half) + w * half, 1.0, 0.0).astype(BF16)
        spread = sum(jnp.dot(part, place, preferred_element_type=F32) for part in logs)
        for out, group in ((own_rows, c), (other_rows, 1 - c)):
            cols = [columns_of(group * heads + h) for h in range(heads)]
            g, o = (
                jnp.concatenate([ref[r, col] for col in cols], axis=0) for ref in (g_ref, o_ref)
            )
            if out is own_rows:
                q = jnp.concatenate([q_ref[r, col] for col in cols], axis=0)
                own[w] = q
                own[2 + w] = g
                own_t[w] = q.T
                own_t[2 + w] = g.T
            mine = head == head_of_lane + group * heads
            row = jnp.sum(jnp.where(mine, spread, 0.0), axis=0, keepdims=True)
            out[w : w + 1, :] = row * LOG2E
            delta = g.astype(F32) * o.astype(F32)
            row = sum(nt(ones, part) for part in split_bf16(delta, 2))
            out[2 + w : 3 + w, :] = row[0:1]
    spot = lax.rem(lax.broadcasted_iota(jnp.int32, (4, lanes), 1), half).astype(F32)
    own_rows[4:8, :] = spot
    other_rows[4:8, :] = spot
    for kind in range(2):
        for w in range(2):
            r = slice(w * half, (w + 1) * half)
            cols = [slice(h * HEAD_SIZE, (h + 1) * HEAD_SIZE) for h in range(heads)]
            x = jnp.concatenate([raw[kind, r, col] for col in cols], axis=0)
            sib[2 * kind + w] = x
            sib_t[2 * kind + w] = x.T
    kv_out[...] = kv[...]


def is_larger(larger, m, b):
    return jnp.max(larger[2 * m + b : 2 * m + b + 1, :]) > 0.5


def one_run(piece, tokens, half, a, which):
    at = a * tokens + which * half
    if not isinstance(which, int):
        at = pl.multiple_of(at, half)
    rows = piece.shape[0] // 2
    return piece[pl.ds(at, half), :], piece[pl.ds(rows + at, half), :]


def kv_grad_kernel(pair, members, larger, own, sib, own_t, sib_t, own_rows, sib_rows, piece, *outs):
    tokens = piece.shape[0] // 4
    half = tokens // 2
    lanes = own.shape[1]
    stacks, turned, vectors = (own, sib), (own_t, sib_t), (own_rows, sib_rows)
    first = [one_run(piece, tokens, half, a, 0) for a in members]
    k, v = (jnp.concatenate(x, axis=0) for x in zip(*first))
    jobs = [(k, v, b, 1, None) for b in range(2)]
    for a in members:
        for b in range(2):
            if pair == 0 and a == b:
                jobs += [(*one_run(piece, tokens, half, a, w), b, w, (a, w)) for w in range(2)]
            else:
                second = is_larger(larger, 2 * pair + a, b)
                which = jnp.where(second, 1, 0)
                run = one_run(piece, tokens, half, a, which)
                jobs.append((*run, b, which, (a, second)))
    if pair == 0:
        key_row = lax.broadcasted_iota(jnp.int32, (half, lanes), 0)
        query_row = lax.rem(lax.broadcasted_iota(jnp.int32, (half, lanes), 1), half)
        seen = key_row <= query_row

    def products(job):
        k, v, b, which, _ = job
        s = jnp.dot(k, turned[b][which], preferred_element_type=F32)
        return s, jnp.dot(v, turned[b][2 + which], preferred_element_type=F32)

    sums = {(a, w): [] for a in members for w in range(2)}
    ahead = products(jobs[0])
    for i, job in enumerate(jobs):
        (s, dp), ahead = ahead, products(jobs[i + 1]) if i + 1 < len(jobs) else None
        _, _, b, which, place = job
        p = jnp.exp2(s * EXP2_SCALE - vectors[b][pl.ds(which, 1), :])
        if place is not None and isinstance(which, int):
            p = jnp.where(seen, p, 0.0)
        ds = (p * (dp - vectors[b][pl.ds(2 + which, 1), :])).astype(BF16)
        value_term = jnp.dot(p.astype(BF16), stacks[b][2 + which], preferred_element_type=F32)
        key_term = jnp.dot(ds, stacks[b][which], preferred_element_type=F32)
        both = key_term, value_term
        if place is None:
            for i, a in enumerate(members):
                sums[a, 0].append([x[i * half : (i + 1) * half] for x in both])
        elif isinstance(which, int):
            sums[place].append(both)
        else:
            a, second = place
            sums[a, 0].append([jnp.where(second, 0.0, x) for x in both])
            sums[a, 1].append([jnp.where(second, x, 0.0) for x in both])
    for (a, w), parts in sums.items():
        i = members.index(a)
        out = outs[i % len(outs)]
        at = w * half + (i * 2 * tokens if len(outs) == 1 else 0)
        out[at : at + half, :] = (sum(x[0] for x in parts) * SCALE).astype(out.dtype)
        at += tokens
        out[at : at + half, :] = sum(x[1] for x in parts).astype(out.dtype)


def q_grads(b, larger, stack, vectors, pieces):
    tokens = pieces[0].shape[0] // 4
    half = tokens // 2
    rows = 2 * tokens
    jobs = {0: [], 1: []}
    columns = vectors[...].T
    spot = columns[:, 4:5]
    for start in range(0, len(pieces), 4):
        some = pieces[start : start + 4]

        def gather(at):
            return jnp.concatenate(
                [x[at + a * tokens : at + a * tokens + half, :] for x in some for a in range(2)],
                axis=0,
            )

        count = 2 * len(some)
        lane = lax.broadcasted_iota(jnp.int32, (1, count * half), 1)
        group = lax.div(lane, half)
        least = [lax.rem(lane, half).astype(F32)] * 2
        for i in range(count):
            m = 2 * start + i
            if m != b:
                sign = jnp.where(is_larger(larger, m, b), 1.0, -1.0) * 2 * tokens
                least[0] = jnp.where(group == i, sign, least[0])
                least[1] = jnp.where(group == i, -sign, least[1])
        runs = [(gather(at), gather(rows + at)) for at in (0, half)]
        jobs[1] += [(1, runs[0], None), (1, runs[1], least[1])]
        jobs[0].append((0, runs[0], least[0]))
    listed = jobs[1] + jobs[0]

    def products(job):
        which, (k, v), _ = job
        return nt(stack[which], k), nt(stack[2 + which], v)

    grad = 0.0
    ahead = products(listed[0])
    for i, (which, (k, _), limit) in enumerate(listed):
        (s, dp), ahead = ahead, products(listed[i + 1]) if i + 1 < len(listed) else None
        p = jnp.exp2(s * EXP2_SCALE - columns[:, which : which + 1])
        if limit is not None:
            p = jnp.where(spot >= limit, p, 0.0)
        ds = (p * (dp - columns[:, 2 + which : 3 + which])).astype(BF16)
        grad = grad + jnp.dot(ds, k, preferred_element_type=F32)
        if i + 1 == len(listed) or listed[i + 1][0] != which:
            yield which, (grad * SCALE).astype(BF16)
            grad = 0.0


def sib_grad_kernel(larger, stack, vectors, *refs):
    pieces, out = refs[:-1], refs[-1]
    for which, grad in q_grads(1, larger, stack, vectors, pieces):
        out[which] = grad


def own_grad_kernel(heads, larger, stack, vectors, other, *refs):
    pieces, (out, held, sems) = refs[:-3], refs[-3:]
    half = out.shape[0] // 2
    c = parity()

    def copies(ref, group):
        return [
            pltpu.make_async_copy(
                ref.at[w, pl.ds(h * half, half), :],
                out.at[pl.ds(w * half, half), columns_of(group * heads + h)],
                sems.at[group_sems + w * heads + h],
            )
            for w in range(2)
            for h in range(heads)
        ]

    group_sems = 0
    first = copies(other, 1 - c)
    group_sems = 2 * heads
    second = copies(held, c)
    for each in first:
        each.start()
    for which, grad in q_grads(0, larger, stack, vectors, pieces):
        held[which] = grad
        for each in second[which * heads : (which + 1) * heads]:
            each.start()
    for each in first + second:
        each.wait()


def merge_kv_kernel(*refs):
    parts, out = refs[:-1], refs[-1]
    tokens = parts[0].shape[0]
    cols = columns_of(parity())
    for i, ref in enumerate(parts):
        out[i * tokens : (i + 1) * tokens, :] = ref[:, cols]


def sum_kernel(*refs):
    parts, outs = refs[:-2], refs[-2:]
    size = outs[0].shape[0]
    for a, out in enumerate(outs):
        value = parts[a][...]
        for part in parts[2:]:
            value = value + part[a * size : (a + 1) * size, :].astype(F32)
        out[...] = value


def share_kernel(tp_count, same, same_last, other, other_last, *refs):
    outs, (total,) = refs[:tp_count], refs[tp_count:]
    tokens = same.shape[0] // 2
    share = tokens // tp_count
    c = parity()
    z = lax.axis_index("tp")
    for ref, last, group in ((same, same_last, c), (other, other_last, 1 - c)):
        total[:, columns_of(group)] = ref[...] + last[...].astype(F32)
    for m, out in enumerate(outs):
        start = jnp.bitwise_xor(z, m) * share
        for kind in range(2):
            r = pl.ds(pl.multiple_of(kind * tokens + start, 8), share)
            out[kind] = total[r, :].astype(BF16)


def spread_kernel(tp_count, order, *refs):
    parts, (key_out, value_out) = refs[:tp_count], refs[tp_count:]
    z = lax.axis_index("tp")
    width = parts[0].shape[2]
    for m, part in zip(order, parts):
        cols = pl.ds(pl.multiple_of(jnp.bitwise_xor(z, m) * width, width), width)
        key_out[:, cols] = part[0]
        value_out[:, cols] = part[1]


def swap(x, axis, shift):
    count = lax.axis_size(axis)
    return lax.ppermute(x, axis, [(i, i ^ shift) for i in range(count)])


def on_device(positions, queries, keys, values, attn_output, output_grad, log_sums):
    n = lax.axis_size("ctx")
    tp_count = lax.axis_size("tp")
    tokens = queries.shape[0]
    half = tokens // 2
    heads = log_sums.shape[1] // 2
    lanes = heads * half

    half_piece = ((2 * tokens, HEAD_SIZE), BF16)
    piece = ((4 * tokens, HEAD_SIZE), BF16)
    stack = ((4, lanes, HEAD_SIZE), BF16)
    other, larger = call(
        pack_q_kernel,
        [((2, tokens, heads * HEAD_SIZE), BF16), ((2 * n, HEAD_SIZE), F32)],
        [],
        [pltpu.SMEM(positions.shape, jnp.int32), pltpu.SemaphoreType.DMA((3,))],
        cost=1.0,
        far=[queries, output_grad, positions],
    )
    pair_keys, pair_values = swap(keys, "ctx", 1), swap(values, "ctx", 1)
    other, pair_keys, pair_values = lax.optimization_barrier((other, pair_keys, pair_values))
    (kv_chip,) = call(merge_kv_kernel, [piece], [keys, pair_keys, values, pair_values])
    raw = swap(other, "ctx", 1)
    turned = ((4, HEAD_SIZE, lanes), BF16)
    vectors = ((8, lanes), F32)
    own_rows, other_rows, own, own_t, sib, sib_t, kv_late = call(
        functools.partial(rows_kernel, heads),
        [vectors, vectors, stack, turned, stack, turned, piece],
        [queries, output_grad, attn_output, log_sums.T, raw, kv_chip],
        cost=1.0,
    )
    sib_rows = swap(other_rows, "ctx", 1)
    late = n // 2 - 1
    pieces = {
        pair: swap(kv_late if pair == late else kv_chip, "ctx", 2 * pair)
        for pair in reversed(range(1, n // 2))
    }
    pieces = [kv_chip] + [pieces[pair] for pair in range(1, n // 2)]

    def kv_grads(pair, outs, members=(0, 1), after=()):
        return call(
            functools.partial(kv_grad_kernel, pair, members),
            outs,
            [larger, own, sib, own_t, sib_t, own_rows, sib_rows, pieces[pair]],
            cost=0.25 * len(members),
            after=after,
        )

    partials = {}
    for pair in reversed(range(1, late)):
        earlier = partials[pair + 1] if pair + 1 < late else []
        partials[pair] = kv_grads(pair, [piece], after=earlier)
    crossing = kv_grads(late, [half_piece], (1,))
    diagonal = kv_grads(late, [half_piece], (0,), crossing) + crossing
    local = kv_grads(0, [(half_piece[0], F32)] * 2, after=diagonal[:1])
    flat = lax.optimization_barrier(tuple(partials[pair][0] for pair in (2, 1)))
    flat = dict(zip((2, 1), flat))
    received = [swap(flat[pair], "ctx", 2 * pair) for pair in (2, 1)]
    last = [swap(x, "ctx", 2 * late + a) for a, x in enumerate(diagonal)]

    sums = ((2 * tokens, HEAD_SIZE), F32)
    sum_same, sum_other = call(sum_kernel, [sums] * 2, [*local, *received])
    sum_pair = swap(sum_other, "ctx", 1)
    (dq_sib,) = call(
        sib_grad_kernel,
        [((2, lanes, HEAD_SIZE), BF16)],
        [larger, sib, sib_rows] + pieces,
        cost=2.5,
        after=[sum_same],
    )
    share = ((2, tokens // tp_count, 2 * HEAD_SIZE), BF16)
    shares = call(
        functools.partial(share_kernel, tp_count),
        [share] * tp_count,
        [sum_same, last[0], sum_pair, last[1]],
        [pltpu.VMEM((2 * tokens, 2 * HEAD_SIZE), F32)],
    )
    dq_sib, *shares = lax.optimization_barrier((dq_sib, *shares))
    dq_other = swap(dq_sib, "ctx", 1)
    (query_grad,) = call(
        functools.partial(own_grad_kernel, heads),
        [(queries.shape, BF16)],
        [larger, own, own_rows, dq_other] + pieces,
        [pltpu.VMEM((2, lanes, HEAD_SIZE), BF16), pltpu.SemaphoreType.DMA((4 * heads,))],
        cost=3.0,
        after=[shares[0]],
        out_spec=HBM,
    )
    order = [0, *range(2, tp_count), 1]
    shares = [shares[0]] + [swap(shares[m], "tp", m) for m in order[1:]]
    final = ((tokens // tp_count, 2 * HEAD_SIZE * tp_count), BF16)
    key_grad, value_grad = call(
        functools.partial(spread_kernel, tp_count, order), [final] * 2, shares, after=[pltpu.with_memory_space_constraint(query_grad, pltpu.HBM)]
    )
    return (query_grad, key_grad, value_grad)


def solution(mesh):
    split = P("ctx", "tp")
    rows = P(("ctx", "tp"), None)
    return jax.shard_map(
        on_device,
        mesh=mesh,
        in_specs=(P(), split, split, split, split, split, split),
        out_specs=(split, rows, rows),
        check_vma=False,
    )
```

```python
import functools
import math

import jax
import jax.numpy as jnp
from jax import lax
from jax.experimental import pallas as pl
from jax.experimental.pallas import tpu as pltpu
from jax.sharding import PartitionSpec as P

HEAD_SIZE = 128
SCALE = 1.0 / math.sqrt(HEAD_SIZE)
EXP2_SCALE = SCALE * math.log2(math.e)
FLOPS_PER_US = 1.1e9
LOG2E = math.log2(math.e)
F32 = jnp.float32
BF16 = jnp.bfloat16
VMEM = pl.BlockSpec(memory_space=pltpu.VMEM)
ANY = pl.BlockSpec(memory_space=pl.ANY)
HBM = pl.BlockSpec(memory_space=pltpu.HBM)
SMEM = pl.BlockSpec(memory_space=pltpu.SMEM)


def call(kernel, outs, ins, scratch=(), smem=0, cost=0.1, far=(), after=(), out_spec=VMEM):
    ins = list(ins) + [pltpu.with_memory_space_constraint(x, pltpu.HBM) for x in far]
    specs = [SMEM] * smem + [VMEM] * (len(ins) - smem - len(far))
    specs += [HBM] * len(far) + [ANY] * len(after)
    moved = sum(x.size * x.dtype.itemsize for x in ins)
    count = len(ins)
    ins = list(ins) + list(after)

    def body(*refs):
        kernel(*refs[:count], *refs[len(ins) :])

    return pl.pallas_call(
        body,
        cost_estimate=pl.CostEstimate(
            flops=int(cost * FLOPS_PER_US), bytes_accessed=moved, transcendentals=0
        ),
        in_specs=specs,
        out_specs=[out_spec] * len(outs),
        out_shape=[jax.ShapeDtypeStruct(shape, dtype) for shape, dtype in outs],
        scratch_shapes=list(scratch),
        compiler_params=pltpu.CompilerParams(vmem_limit_bytes=48 * 2**20),
    )(*ins)


def nt(a, b):
    return lax.dot_general(a, b, (((1,), (1,)), ((), ())), preferred_element_type=F32)


def parity():
    return lax.rem(lax.axis_index("ctx"), 2)


def columns_of(head):
    return pl.ds(pl.multiple_of(head * HEAD_SIZE, HEAD_SIZE), HEAD_SIZE)


def copy_all(pairs, sems):
    copies = [
        pltpu.make_async_copy(src, dst, sems.at[i]) for i, (src, dst) in enumerate(pairs)
    ]
    for each in copies:
        each.start()
    for each in copies:
        each.wait()


def run_starts(pos_ref, tokens, shift):
    ctx = lax.axis_index("ctx")
    return pos_ref[jnp.bitwise_xor(ctx, shift) * tokens]


def pack_q_kernel(q_hbm, g_hbm, pos_hbm, out, larger, pos, sems):
    tokens, width = q_hbm.shape[0], out.shape[2]
    cols = pl.ds(pl.multiple_of((1 - parity()) * width, width), width)
    pairs = [(pos_hbm, pos), (q_hbm.at[:, cols], out.at[0]), (g_hbm.at[:, cols], out.at[1])]
    copy_all(pairs, sems)
    for m in range(larger.shape[0] // 2):
        for b in range(2):
            flag = jnp.where(run_starts(pos, tokens, m) > run_starts(pos, tokens, b), 1.0, 0.0)
            larger[2 * m + b : 2 * m + b + 1, :] = jnp.full((1, HEAD_SIZE), flag, F32)


def split_bf16(x, terms):
    parts = []
    for _ in range(terms):
        part = x.astype(BF16)
        parts.append(part)
        x = x - part.astype(F32)
    return parts


def rows_kernel(heads, q_ref, g_ref, o_ref, log, raw, kv, *refs):
    own_rows, other_rows, own, own_t, sib, sib_t, kv_out = refs
    lanes = own.shape[1]
    half = lanes // heads
    c = parity()
    ones = jnp.ones((8, HEAD_SIZE), BF16)
    groups, tokens = log.shape
    token = lax.broadcasted_iota(jnp.int32, (tokens, lanes), 0)
    lane = lax.broadcasted_iota(jnp.int32, (tokens, lanes), 1)
    head = lax.broadcasted_iota(jnp.int32, (groups, lanes), 0)
    head_of_lane = lax.div(lax.broadcasted_iota(jnp.int32, (groups, lanes), 1), half)
    logs = split_bf16(jnp.clip(log[...], -1e30, 1e30), 3)
    for w in range(2):
        r = slice(w * half, (w + 1) * half)
        place = jnp.where(token == lax.rem(lane, half) + w * half, 1.0, 0.0).astype(BF16)
        spread = sum(jnp.dot(part, place, preferred_element_type=F32) for part in logs)
        for out, group in ((own_rows, c), (other_rows, 1 - c)):
            cols = [columns_of(group * heads + h) for h in range(heads)]
            g, o = (
                jnp.concatenate([ref[r, col] for col in cols], axis=0) for ref in (g_ref, o_ref)
            )
            if out is own_rows:
                q = jnp.concatenate([q_ref[r, col] for col in cols], axis=0)
                own[w] = q
                own[2 + w] = g
                own_t[w] = q.T
                own_t[2 + w] = g.T
            mine = head == head_of_lane + group * heads
            row = jnp.sum(jnp.where(mine, spread, 0.0), axis=0, keepdims=True)
            out[w : w + 1, :] = row * LOG2E
            delta = g.astype(F32) * o.astype(F32)
            row = sum(nt(ones, part) for part in split_bf16(delta, 2))
            out[2 + w : 3 + w, :] = row[0:1]
    spot = lax.rem(lax.broadcasted_iota(jnp.int32, (4, lanes), 1), half).astype(F32)
    own_rows[4:8, :] = spot
    other_rows[4:8, :] = spot
    for kind in range(2):
        for w in range(2):
            r = slice(w * half, (w + 1) * half)
            cols = [slice(h * HEAD_SIZE, (h + 1) * HEAD_SIZE) for h in range(heads)]
            x = jnp.concatenate([raw[kind, r, col] for col in cols], axis=0)
            sib[2 * kind + w] = x
            sib_t[2 * kind + w] = x.T
    kv_out[...] = kv[...]


def is_larger(larger, m, b):
    return jnp.max(larger[2 * m + b : 2 * m + b + 1, :]) > 0.5


def one_run(piece, tokens, half, a, which):
    at = a * tokens + which * half
    if not isinstance(which, int):
        at = pl.multiple_of(at, half)
    rows = piece.shape[0] // 2
    return piece[pl.ds(at, half), :], piece[pl.ds(rows + at, half), :]


def kv_grad_kernel(pair, members, larger, own, sib, own_t, sib_t, own_rows, sib_rows, piece, *outs):
    tokens = piece.shape[0] // 4
    half = tokens // 2
    lanes = own.shape[1]
    stacks, turned, vectors = (own, sib), (own_t, sib_t), (own_rows, sib_rows)
    first = [one_run(piece, tokens, half, a, 0) for a in members]
    k, v = (jnp.concatenate(x, axis=0) for x in zip(*first))
    jobs = [(k, v, b, 1, None) for b in range(2)]
    for a in members:
        for b in range(2):
            if pair == 0 and a == b:
                jobs += [(*one_run(piece, tokens, half, a, w), b, w, (a, w)) for w in range(2)]
            else:
                second = is_larger(larger, 2 * pair + a, b)
                which = jnp.where(second, 1, 0)
                run = one_run(piece, tokens, half, a, which)
                jobs.append((*run, b, which, (a, second)))
    if pair == 0:
        key_row = lax.broadcasted_iota(jnp.int32, (half, lanes), 0)
        query_row = lax.rem(lax.broadcasted_iota(jnp.int32, (half, lanes), 1), half)
        seen = key_row <= query_row

    def products(job):
        k, v, b, which, _ = job
        s = jnp.dot(k, turned[b][which], preferred_element_type=F32)
        return s, jnp.dot(v, turned[b][2 + which], preferred_element_type=F32)

    sums = {(a, w): [] for a in members for w in range(2)}
    ahead = products(jobs[0])
    for i, job in enumerate(jobs):
        (s, dp), ahead = ahead, products(jobs[i + 1]) if i + 1 < len(jobs) else None
        _, _, b, which, place = job
        p = jnp.exp2(s * EXP2_SCALE - vectors[b][pl.ds(which, 1), :])
        if place is not None and isinstance(which, int):
            p = jnp.where(seen, p, 0.0)
        ds = (p * (dp - vectors[b][pl.ds(2 + which, 1), :])).astype(BF16)
        value_term = jnp.dot(p.astype(BF16), stacks[b][2 + which], preferred_element_type=F32)
        key_term = jnp.dot(ds, stacks[b][which], preferred_element_type=F32)
        both = key_term, value_term
        if place is None:
            for i, a in enumerate(members):
                sums[a, 0].append([x[i * half : (i + 1) * half] for x in both])
        elif isinstance(which, int):
            sums[place].append(both)
        else:
            a, second = place
            sums[a, 0].append([jnp.where(second, 0.0, x) for x in both])
            sums[a, 1].append([jnp.where(second, x, 0.0) for x in both])
    for (a, w), parts in sums.items():
        i = members.index(a)
        out = outs[i % len(outs)]
        at = w * half + (i * 2 * tokens if len(outs) == 1 else 0)
        out[at : at + half, :] = (sum(x[0] for x in parts) * SCALE).astype(out.dtype)
        at += tokens
        out[at : at + half, :] = sum(x[1] for x in parts).astype(out.dtype)


def q_grads(b, larger, stack, vectors, pieces):
    tokens = pieces[0].shape[0] // 4
    half = tokens // 2
    rows = 2 * tokens
    jobs = {0: [], 1: []}
    columns = vectors[...].T
    spot = columns[:, 4:5]
    for start in range(0, len(pieces), 4):
        some = pieces[start : start + 4]

        def gather(at):
            return jnp.concatenate(
                [x[at + a * tokens : at + a * tokens + half, :] for x in some for a in range(2)],
                axis=0,
            )

        count = 2 * len(some)
        lane = lax.broadcasted_iota(jnp.int32, (1, count * half), 1)
        group = lax.div(lane, half)
        least = [lax.rem(lane, half).astype(F32)] * 2
        for i in range(count):
            m = 2 * start + i
            if m != b:
                sign = jnp.where(is_larger(larger, m, b), 1.0, -1.0) * 2 * tokens
                least[0] = jnp.where(group == i, sign, least[0])
                least[1] = jnp.where(group == i, -sign, least[1])
        runs = [(gather(at), gather(rows + at)) for at in (0, half)]
        jobs[1] += [(1, runs[0], None), (1, runs[1], least[1])]
        jobs[0].append((0, runs[0], least[0]))
    listed = jobs[1] + jobs[0]

    def products(job):
        which, (k, v), _ = job
        return nt(stack[which], k), nt(stack[2 + which], v)

    grad = 0.0
    ahead = products(listed[0])
    for i, (which, (k, _), limit) in enumerate(listed):
        (s, dp), ahead = ahead, products(listed[i + 1]) if i + 1 < len(listed) else None
        p = jnp.exp2(s * EXP2_SCALE - columns[:, which : which + 1])
        if limit is not None:
            p = jnp.where(spot >= limit, p, 0.0)
        ds = (p * (dp - columns[:, 2 + which : 3 + which])).astype(BF16)
        grad = grad + jnp.dot(ds, k, preferred_element_type=F32)
        if i + 1 == len(listed) or listed[i + 1][0] != which:
            yield which, (grad * SCALE).astype(BF16)
            grad = 0.0


def sib_grad_kernel(larger, stack, vectors, *refs):
    pieces, out = refs[:-1], refs[-1]
    for which, grad in q_grads(1, larger, stack, vectors, pieces):
        out[which] = grad


def own_grad_kernel(heads, larger, stack, vectors, other, *refs):
    pieces, (out, held, sems) = refs[:-3], refs[-3:]
    half = out.shape[0] // 2
    c = parity()

    def copies(ref, group):
        return [
            pltpu.make_async_copy(
                ref.at[w, pl.ds(h * half, half), :],
                out.at[pl.ds(w * half, half), columns_of(group * heads + h)],
                sems.at[group_sems + w * heads + h],
            )
            for w in range(2)
            for h in range(heads)
        ]

    group_sems = 0
    first = copies(other, 1 - c)
    group_sems = 2 * heads
    second = copies(held, c)
    for each in first:
        each.start()
    for which, grad in q_grads(0, larger, stack, vectors, pieces):
        held[which] = grad
        for each in second[which * heads : (which + 1) * heads]:
            each.start()
    for each in first + second:
        each.wait()


def merge_kv_kernel(*refs):
    parts, out = refs[:-1], refs[-1]
    tokens = parts[0].shape[0]
    cols = columns_of(parity())
    for i, ref in enumerate(parts):
        out[i * tokens : (i + 1) * tokens, :] = ref[:, cols]


def sum_kernel(*refs):
    parts, outs = refs[:-2], refs[-2:]
    size = outs[0].shape[0]
    for a, out in enumerate(outs):
        value = parts[a][...]
        for part in parts[2:]:
            value = value + part[a * size : (a + 1) * size, :].astype(F32)
        out[...] = value


def share_kernel(tp_count, same, same_last, other, other_last, *refs):
    outs, (total,) = refs[:tp_count], refs[tp_count:]
    tokens = same.shape[0] // 2
    share = tokens // tp_count
    c = parity()
    z = lax.axis_index("tp")
    for ref, last, group in ((same, same_last, c), (other, other_last, 1 - c)):
        total[:, columns_of(group)] = ref[...] + last[...].astype(F32)
    for m, out in enumerate(outs):
        start = jnp.bitwise_xor(z, m) * share
        for kind in range(2):
            r = pl.ds(pl.multiple_of(kind * tokens + start, 8), share)
            out[kind] = total[r, :].astype(BF16)


def spread_kernel(tp_count, order, *refs):
    parts, (key_out, value_out) = refs[:tp_count], refs[tp_count:]
    z = lax.axis_index("tp")
    width = parts[0].shape[2]
    for m, part in zip(order, parts):
        cols = pl.ds(pl.multiple_of(jnp.bitwise_xor(z, m) * width, width), width)
        key_out[:, cols] = part[0]
        value_out[:, cols] = part[1]


def swap(x, axis, shift):
    count = lax.axis_size(axis)
    return lax.ppermute(x, axis, [(i, i ^ shift) for i in range(count)])


def on_device(positions, queries, keys, values, attn_output, output_grad, log_sums):
    n = lax.axis_size("ctx")
    tp_count = lax.axis_size("tp")
    tokens = queries.shape[0]
    half = tokens // 2
    heads = log_sums.shape[1] // 2
    lanes = heads * half

    half_piece = ((2 * tokens, HEAD_SIZE), BF16)
    piece = ((4 * tokens, HEAD_SIZE), BF16)
    stack = ((4, lanes, HEAD_SIZE), BF16)
    other, larger = call(
        pack_q_kernel,
        [((2, tokens, heads * HEAD_SIZE), BF16), ((2 * n, HEAD_SIZE), F32)],
        [],
        [pltpu.SMEM(positions.shape, jnp.int32), pltpu.SemaphoreType.DMA((3,))],
        cost=1.0,
        far=[queries, output_grad, positions],
    )
    pair_keys, pair_values = swap(keys, "ctx", 1), swap(values, "ctx", 1)
    other, pair_keys, pair_values = lax.optimization_barrier((other, pair_keys, pair_values))
    (kv_chip,) = call(merge_kv_kernel, [piece], [keys, pair_keys, values, pair_values])
    raw = swap(other, "ctx", 1)
    turned = ((4, HEAD_SIZE, lanes), BF16)
    vectors = ((8, lanes), F32)
    own_rows, other_rows, own, own_t, sib, sib_t, kv_late = call(
        functools.partial(rows_kernel, heads),
        [vectors, vectors, stack, turned, stack, turned, piece],
        [queries, output_grad, attn_output, log_sums.T, raw, kv_chip],
        cost=1.0,
    )
    sib_rows = swap(other_rows, "ctx", 1)
    late = n // 2 - 1
    pieces = {
        pair: swap(kv_late if pair == late else kv_chip, "ctx", 2 * pair)
        for pair in reversed(range(1, n // 2))
    }
    pieces = [kv_chip] + [pieces[pair] for pair in range(1, n // 2)]

    def kv_grads(pair, outs, members=(0, 1), after=()):
        return call(
            functools.partial(kv_grad_kernel, pair, members),
            outs,
            [larger, own, sib, own_t, sib_t, own_rows, sib_rows, pieces[pair]],
            cost=0.25 * len(members),
            after=after,
        )

    partials = {}
    for pair in reversed(range(1, late)):
        earlier = partials[pair + 1] if pair + 1 < late else []
        partials[pair] = kv_grads(pair, [piece], after=earlier)
    crossing = kv_grads(late, [half_piece], (1,))
    diagonal = kv_grads(late, [half_piece], (0,), crossing) + crossing
    local = kv_grads(0, [(half_piece[0], F32)] * 2, after=diagonal[:1])
    back = list(reversed(range(1, late)))
    sent = lax.optimization_barrier(tuple(partials[pair][0] for pair in back))
    received = [swap(x, "ctx", 2 * pair) for pair, x in zip(back, sent)]
    last = [swap(x, "ctx", 2 * late + a) for a, x in enumerate(diagonal)]

    sums = ((2 * tokens, HEAD_SIZE), F32)
    sum_same, sum_other = call(sum_kernel, [sums] * 2, [*local, *received])
    sum_pair = swap(sum_other, "ctx", 1)
    (dq_sib,) = call(
        sib_grad_kernel,
        [((2, lanes, HEAD_SIZE), BF16)],
        [larger, sib, sib_rows] + pieces,
        cost=2.5,
        after=[sum_same],
    )
    share = ((2, tokens // tp_count, 2 * HEAD_SIZE), BF16)
    shares = call(
        functools.partial(share_kernel, tp_count),
        [share] * tp_count,
        [sum_same, last[0], sum_pair, last[1]],
        [pltpu.VMEM((2 * tokens, 2 * HEAD_SIZE), F32)],
    )
    dq_sib, *shares = lax.optimization_barrier((dq_sib, *shares))
    dq_other = swap(dq_sib, "ctx", 1)
    (query_grad,) = call(
        functools.partial(own_grad_kernel, heads),
        [(queries.shape, BF16)],
        [larger, own, own_rows, dq_other] + pieces,
        [pltpu.VMEM((2, lanes, HEAD_SIZE), BF16), pltpu.SemaphoreType.DMA((4 * heads,))],
        cost=3.0,
        after=[shares[0]],
        out_spec=HBM,
    )
    order = [0, *range(2, tp_count), 1]
    shares = [shares[0]] + [swap(shares[m], "tp", m) for m in order[1:]]
    final = ((tokens // tp_count, 2 * HEAD_SIZE * tp_count), BF16)
    key_grad, value_grad = call(
        functools.partial(spread_kernel, tp_count, order), [final] * 2, shares, after=[pltpu.with_memory_space_constraint(query_grad, pltpu.HBM)]
    )
    return (query_grad, key_grad, value_grad)


def solution(mesh):
    split = P("ctx", "tp")
    rows = P(("ctx", "tp"), None)
    return jax.shard_map(
        on_device,
        mesh=mesh,
        in_specs=(P(), split, split, split, split, split, split),
        out_specs=(split, rows, rows),
        check_vma=False,
    )
```
